128 devices in a mesh: dp: 8 (over z, core), mp: 16 (over x, y).
Axes of the slice: x: 4, y: 4, z: 4, core: 2. Of those that a mesh axis runs over, the one named last changes fastest.
Arguments:
- inputs: bfloat16 [3072, 4096], P('dp'), may hold values from -6 to 6
- grad_out: bfloat16 [3072, 22016], P('dp', 'mp'), may hold values from -0.3125 to 0.3125
- error: bfloat16 [8, 4096, 22016], P('dp', None, 'mp'), may hold values from -6 to 6
- q_prev: float32 [22016, 32], P('mp'), may hold values from -6 to 6
Outputs:
- new_error: bfloat16 [8, 4096, 22016], P('dp', None, 'mp')
- q_new: float32 [22016, 32], P('mp')
The draws below stay inside these ranges and needn't reach their ends.
All inputs are finite; a program needn't handle non-finite values.
Results may differ from the reference program's by a relative error of at most 0.001.
Values sent between devices are 32-bit elements; how exact they have to be, the bound alone decides.
A program may use at most 128 MiB of HBM per device.

```python
import jax
import jax.numpy as jnp
from jax import lax

DW = 4096
FF = 22016
RANK = 32
ITERS = 2
ROWS_DEV = 384
ROWS = 3072
N_DP = 8


def block_levels(rng, dims, shards, smallest, high):
    level = 1.0
    for position, parts in shards:
        steps = jax.random.uniform(jax.random.fold_in(jax.random.fold_in(rng, 6), position), (parts,), jnp.float32, smallest / len(shards), high / len(shards))
        level = level * jnp.repeat(jnp.exp(steps), dims[position] // parts).reshape((-1,) + (1,) * (len(dims) - 1 - position))
    return level


def normal_values(key, dims, scale, reach, shards=(), dtype=jnp.bfloat16):
    loudness = block_levels(key, dims, shards, -0.22, 0.18) if shards else 1.0
    result = jax.random.normal(key, dims, jnp.float32) * scale * loudness
    return jnp.minimum(jnp.maximum(result, -reach), reach).astype(dtype)


def setup_inputs(seed: int = 0) -> dict:
    arg_keys = jax.random.split(jax.random.key(seed), 5)
    inputs = normal_values(arg_keys[0], (ROWS, DW), 1.0, 6.0, ((0, 8),))
    grad_out = normal_values(arg_keys[1], (ROWS, FF), ROWS_DEV ** -0.5, 0.3125, ((0, 8), (1, 16)))
    error = normal_values(arg_keys[2], (N_DP, DW, FF), 1.0, 6.0, ((0, 8), (2, 16)))
    q_prev = normal_values(arg_keys[3], (FF, RANK), 1.0, 6.0, ((0, 16),), jnp.float32)
    return dict(inputs=inputs, grad_out=grad_out, error=error, q_prev=q_prev)


def orthonormal(left):
    gram = jnp.dot(left.T, left, precision=lax.Precision.HIGHEST)
    lower = jnp.linalg.cholesky(gram)
    return lax.linalg.triangular_solve(lower, left, left_side=False, lower=True, transpose_a=True)

def reference(inputs, grad_out, error, q_prev):
    xs = inputs.reshape(N_DP, ROWS_DEV, DW)
    gs = grad_out.reshape(N_DP, ROWS_DEV, FF)

    def build(items):
        grad = lax.dot_general(items[0].astype(jnp.float32), items[1].astype(jnp.float32), (((0,), (0,)), ((), ())), preferred_element_type=jnp.float32)
        return grad + items[2].astype(jnp.float32)
    merged = lax.map(build, (xs, gs, error))
    factor = q_prev
    p_hat = jnp.zeros((DW, RANK), jnp.float32)
    for step in range(ITERS):
        left = jnp.einsum('rdf,fk->dk', merged, factor, precision=lax.Precision.HIGHEST)
        p_hat = orthonormal(left)
        factor = jnp.einsum('rdf,dk->fk', merged, p_hat, precision=lax.Precision.HIGHEST) / N_DP
    approx = jnp.dot(p_hat, factor.T, precision=lax.Precision.HIGHEST)
    new_error = lax.map(lambda block: (block - approx).astype(jnp.bfloat16), merged)
    return (new_error, factor)
```

```python
import jax
import jax.numpy as jnp
from jax import lax
from jax.experimental import pallas as pl
from jax.experimental.pallas import tpu as pltpu
from jax.sharding import PartitionSpec as P

MESH = pl.DeviceIdType.MESH
BF, F32 = jnp.bfloat16, jnp.float32
ITERS = 2
UNIT = 512
HALF = 768


def dot(a, b, ca, cb):
    return lax.dot_general(a, b, (((ca,), (cb,)), ((), ())), preferred_element_type=F32)


def exact(a, b, ca, cb):
    return lax.dot_general(
        a, b, (((ca,), (cb,)), ((), ())), precision=lax.Precision.HIGHEST, preferred_element_type=F32
    )


def split(v):
    hi = v.astype(BF)
    rest = v - hi.astype(F32)
    mid = rest.astype(BF)
    low = (rest - mid.astype(F32)).astype(BF)
    return jnp.concatenate([hi, mid, low], axis=0)


def fold(v):
    r = v.shape[0] // 3
    return v[:r] + (v[r : 2 * r] + v[2 * r :])


def inverse_factor(gram):
    r = gram.shape[0]
    row = lax.broadcasted_iota(jnp.int32, (r, 2 * r), 0)
    col = lax.broadcasted_iota(jnp.int32, (r, 2 * r), 1)
    eye = (row == col)[:, :r].astype(F32)
    a = jnp.concatenate([gram, eye], axis=1)
    for j in range(r):
        factor = a[:, j : j + 1] / a[j : j + 1, j : j + 1]
        a = a - jnp.where(row > j, factor, 0.0) * a[j : j + 1, :]
    pivots = jnp.sum(jnp.where(row == col, a, 0.0), axis=1, keepdims=True)
    return a[:, r:] * lax.rsqrt(pivots)


def factors_kernel(
    x_h, y_h, e_h, q0, left_o, right_o, qt_o,
    x, y, e, qs, xq, wacc, sacc, linv,
    pout, pin, pown, slots, pt, wloc, wrx, wz, wfull,
    in_sem, e_sem, cx_s, cx_r, rs_s, rs_r, ag_s, ag_r, fw_s, fw_r, wx_s, wx_r, wz_s, wz_r, wf_s, wf_r,
):
    dp, mp = lax.axis_index("dp"), lax.axis_index("mp")
    z, c = dp // 2, dp % 2
    px, py = mp // 4, mp % 4
    ff = y.shape[0]
    rest = ff - HALF
    partner = (z * 2 + 1 - c, mp)

    def chip(dx, dy, dz):
        return (((z + dz) % 4) * 2 + c, ((px + dx) % 4) * 4 + (py + dy) % 4)

    def far_first(i):
        return (2 + i + i // 2 + 2 * (i // 3)) % 4

    def rows(half, u):
        return pl.ds(pl.multiple_of(half * 2048 + u * UNIT, UNIT), UNIT)

    def remote(src, dst, ss, rs, to):
        return pltpu.make_async_remote_copy(src, dst, ss, rs, device_id=to, device_id_type=MESH)

    def arrived(ref, sem):
        pltpu.make_async_copy(ref, ref, sem).wait()

    barrier = pltpu.get_barrier_semaphore()

    def greet(k, carry):
        pl.semaphore_signal(barrier, inc=1, device_id=chip(k // 16, (k // 4) % 4, k % 4), device_id_type=MESH)
        return carry

    lax.fori_loop(1, 64, greet, 0)
    pl.semaphore_signal(barrier, inc=1, device_id=partner, device_id_type=MESH)

    loads = [
        pltpu.make_async_copy(y_h, y, in_sem.at[0]),
        pltpu.make_async_copy(x_h, x, in_sem.at[1]),
    ]
    for load in loads:
        load.start()

    def e_load(k):
        half = (1 - c) * (1 - k // 4) + c * (k // 4)
        at = rows(half, (px + far_first(k % 4)) % 4)
        return pltpu.make_async_copy(e_h.at[0, :, at], e.at[:, at], e_sem.at[k])

    def start_load(k, carry):
        e_load(k).start()
        return carry

    lax.fori_loop(0, 8, start_load, 0)

    wloc[...] = jnp.zeros_like(wloc)
    qs[...] = split(q0[...])
    loads[0].wait()
    loads[1].wait()
    pl.semaphore_wait(barrier, 64)

    def iteration(it, carry):
        xq[...] = split(fold(dot(qs[...], y[...], 1, 0)))

        def term(half, u):
            at = rows(half, u)
            return fold(dot(qs[...], e[:, at], 1, 0) + dot(xq[...], x[:, at], 1, 0))

        def other_half(i, carry):
            @pl.when(it == 0)
            def _():
                e_load(i).wait()

            u = (px + far_first(i)) % 4
            v = term(1 - c, u)
            for t in range(4):
                pout[it, i, t] = v[:, 128 * t : 128 * t + 128]
            remote(pout.at[it, i], pin.at[it, i], cx_s.at[it], cx_r.at[it, i], partner).start()
            return carry

        lax.fori_loop(0, 4, other_half, 0)

        def own_half(i, carry):
            @pl.when(it == 0)
            def _():
                e_load(i + 4).wait()

            dx = far_first(i)
            u = (px + dx) % 4
            v = term(c, u)
            arrived(pin.at[it, i], cx_r.at[it, i])
            for t in range(4):
                pown[it, u, t] = v[:, 128 * t : 128 * t + 128] + pin[it, i, t]

            def send(j, carry):
                dy, dz = j // 4, j % 4
                src = pown.at[it, u, (py + dy) % 4, pl.ds(pl.multiple_of(((z + dz) % 4) * 8, 8), 8), :]
                remote(src, slots.at[it, dx * 16 + j], rs_s.at[it], rs_r.at[it], chip(dx, dy, dz)).start()
                return carry

            lax.fori_loop(i // 3, 16, send, 0)
            return carry

        lax.fori_loop(0, 4, own_half, 0)

        mine = pl.ds(pl.multiple_of(z * 8, 8), 8)
        slots[it, 0] = pown[it, px, py, mine, :]
        arrived(slots.at[it, pl.ds(1, 63)], rs_r.at[it])
        pt[it, c, px * 4 + py, mine, :] = jnp.sum(slots[it], axis=0)

        def spread(k, carry):
            dx, dy, dz = far_first(k // 16), (k // 4) % 4, k % 4
            tile = pt.at[it, c, px * 4 + py, mine, :]
            remote(tile, tile, ag_s.at[it], ag_r.at[it, dx], chip(dx, dy, dz)).start()
            return carry

        lax.fori_loop(0, 48, spread, 0)
        lax.fori_loop(49, 64, spread, 0)

        wacc[...] = jnp.zeros_like(wacc)
        sacc[...] = jnp.zeros_like(sacc)

        def unit(half, u):
            at = rows(half, u)
            p = split(jnp.concatenate([pt[it, half, u * 4 + t] for t in range(4)], axis=1))
            wacc[...] += dot(p, e[:, at], 1, 1)
            sacc[...] += dot(p, x[:, at], 1, 1)

        def near(i):
            return (px + 4 - far_first(3 - i)) % 4

        def gather(i, carry):
            u = near(i)

            @pl.when(i == 0)
            def _():
                arrived(slots.at[it, pl.ds(0, 15)], ag_r.at[it, 0])

            @pl.when(i > 0)
            def _():
                arrived(slots.at[it, pl.ds(0, 16)], ag_r.at[it, far_first(3 - i)])

            block = pt.at[it, c, pl.ds(u * 4, 4)]
            remote(block, block, fw_s.at[it], fw_r.at[it, i], partner).start()
            unit(c, u)

            @pl.when(i > 0)
            def _():
                v = near(i - 1)
                arrived(pt.at[it, 1 - c, pl.ds(v * 4, 4)], fw_r.at[it, i - 1])
                unit(1 - c, v)

            return carry

        lax.fori_loop(0, 4, gather, 0)
        v = near(3)
        arrived(pt.at[it, 1 - c, pl.ds(v * 4, 4)], fw_r.at[it, 3])
        unit(1 - c, v)

        w = fold(wacc[...] + dot(split(fold(sacc[...])), y[...], 1, 1))
        wloc[it, 0] = w[:, :HALF]
        wloc[it, 1, :, :rest] = w[:, HALF:]
        remote(wloc.at[it, 1 - c], wrx.at[it], wx_s.at[it], wx_r.at[it], partner).start()
        arrived(wrx.at[it], wx_r.at[it])
        wz[it, z] = wloc[it, c] + wrx[it]
        for dz in (2, 1, 3):
            remote(wz.at[it, z], wz.at[it, z], wz_s.at[it], wz_r.at[it, dz], chip(0, 0, dz)).start()

        gram = jnp.zeros((96, 96), F32)

        def add_gram(k, total):
            p = split(jnp.concatenate([pt[it, k // 4, (k % 4) * 4 + t] for t in range(4)], axis=1))
            return total + dot(p, p, 1, 1)

        gram = fold(lax.fori_loop(0, 8, add_gram, gram))
        gram = gram[:, :32] + (gram[:, 32:64] + gram[:, 64:])
        linv[...] = inverse_factor(gram)

        @pl.when(it == ITERS - 1)
        def _():
            def write_left(k, carry):
                p = jnp.concatenate([pt[it, k // 4, (k % 4) * 4 + t] for t in range(4)], axis=1)
                p = split(-exact(linv[...], p, 1, 0))
                left_o[:, rows(0, k)] = jnp.concatenate([p[:32], p[:32], p[32:64], p[32:64]], axis=0)
                return carry

            lax.fori_loop(0, 8, write_left, 0)

        for dz in (1, 3, 2):
            arrived(wz.at[it, (z + 4 - dz) % 4], wz_r.at[it, dz])
        wfull[it, c] = ((wz[it, 0] + wz[it, 1]) + wz[it, 2]) + wz[it, 3]
        remote(wfull.at[it, c], wfull.at[it, c], wf_s.at[it], wf_r.at[it], partner).start()
        arrived(wfull.at[it, 1 - c], wf_r.at[it])
        scale = 0.125 * linv[...]
        first, second = exact(scale, wfull[it, 0], 1, 0), exact(scale, wfull[it, 1], 1, 0)[:, :rest]
        qs[:, :HALF] = split(first)
        qs[:, HALF:] = split(second)

        @pl.when(it == ITERS - 1)
        def _():
            qt_o[:, :HALF] = first
            qt_o[:, HALF:] = second

        arrived(pout.at[it], cx_s.at[it])
        arrived(slots.at[it, pl.ds(1, 63)], rs_s.at[it])
        arrived(slots.at[it, pl.ds(1, 63)], ag_s.at[it])
        arrived(pt.at[it, c], fw_s.at[it])
        arrived(wrx.at[it], wx_s.at[it])
        arrived(wz.at[it, pl.ds(0, 3)], wz_s.at[it])
        arrived(wfull.at[it, c], wf_s.at[it])
        return carry

    lax.fori_loop(0, ITERS, iteration, 0)
    right = qs[:64].astype(F32)
    right_o[...] = jnp.transpose(jnp.concatenate([right, right], axis=0)).astype(BF)


def error_kernel(e, x, left, y, right, qt, out, q_out):
    k = jnp.concatenate([y[...], right[...]], axis=1)
    r = jnp.concatenate([x[...], left[...]], axis=0)
    out[0] = (e[0].astype(F32) + dot(k, r, 1, 0)).astype(BF)

    @pl.when(pl.program_id(0) == 0)
    def _():
        q_out[...] = qt[...]


def local(inputs, grad_out, error, q_prev):
    grad_out, q_prev, error = grad_out.T, q_prev.T, jnp.swapaxes(error, 1, 2)
    tokens, dw = inputs.shape
    rank, ff = q_prev.shape
    vmem = pl.BlockSpec(memory_space=pltpu.VMEM)
    dma = pltpu.SemaphoreType.DMA
    left, right, qt = pl.pallas_call(
        factors_kernel,
        out_shape=(
            jax.ShapeDtypeStruct((4 * rank, dw), BF),
            jax.ShapeDtypeStruct((ff, 4 * rank), BF),
            jax.ShapeDtypeStruct((rank, ff), F32),
        ),
        in_specs=[pl.BlockSpec(memory_space=pl.ANY)] * 3 + [vmem],
        out_specs=(vmem,) * 3,
        scratch_shapes=[
            pltpu.VMEM((tokens, dw), BF),
            pltpu.VMEM((ff, tokens), BF),
            pltpu.VMEM((ff, dw), BF),
            pltpu.VMEM((3 * rank, ff), BF),
            pltpu.VMEM((3 * rank, tokens), BF),
            pltpu.VMEM((3 * rank, ff), F32),
            pltpu.VMEM((3 * rank, tokens), F32),
            pltpu.VMEM((rank, rank), F32),
            pltpu.VMEM((2, 4, 4, rank, 128), F32),
            pltpu.VMEM((2, 4, 4, rank, 128), F32),
            pltpu.VMEM((2, 4, 4, rank, 128), F32),
            pltpu.VMEM((2, 64, 8, 128), F32),
            pltpu.VMEM((2, 2, 16, rank, 128), F32),
            pltpu.VMEM((2, 2, rank, HALF), F32),
            pltpu.VMEM((2, rank, HALF), F32),
            pltpu.VMEM((2, 4, rank, HALF), F32),
            pltpu.VMEM((2, 2, rank, HALF), F32),
            dma((2,)), dma((8,)),
            dma((2,)), dma((2, 4)),
            dma((2,)), dma((2,)),
            dma((2,)), dma((2, 4)),
            dma((2,)), dma((2, 4)),
            dma((2,)), dma((2,)),
            dma((2,)), dma((2, 4)),
            dma((2,)), dma((2,)),
        ],
        compiler_params=pltpu.CompilerParams(
            collective_id=0, has_side_effects=True, vmem_limit_bytes=40 * 2**20
        ),
        name="power_iterations",
    )(inputs, grad_out, error, q_prev)
    step = 512
    new_error, q_new = pl.pallas_call(
        error_kernel,
        grid=(dw // step,),
        out_shape=(jax.ShapeDtypeStruct(error.shape, BF), jax.ShapeDtypeStruct((rank, ff), F32)),
        in_specs=[
            pl.BlockSpec((1, ff, step), lambda i: (0, 0, i)),
            pl.BlockSpec((tokens, step), lambda i: (0, i)),
            pl.BlockSpec((4 * rank, step), lambda i: (0, i)),
            pl.BlockSpec((ff, tokens), lambda i: (0, 0)),
            pl.BlockSpec((ff, 4 * rank), lambda i: (0, 0)),
            pl.BlockSpec((rank, ff), lambda i: (0, 0)),
        ],
        out_specs=(
            pl.BlockSpec((1, ff, step), lambda i: (0, 0, i)),
            pl.BlockSpec((rank, ff), lambda i: (0, 0)),
        ),
        compiler_params=pltpu.CompilerParams(vmem_limit_bytes=32 * 2**20),
        name="new_error",
    )(error, inputs, left, grad_out, right, qt)
    return jnp.swapaxes(new_error, 1, 2), q_new.T


def solution(mesh):
    placed = (P("dp", None), P("dp", "mp"), P("dp", None, "mp"), P("mp", None))
    return jax.shard_map(
        local,
        mesh=mesh,
        in_specs=placed,
        out_specs=(P("dp", None, "mp"), P("mp", None)),
        check_vma=False,
    )
```

```python
import jax
import jax.numpy as jnp
from jax import lax
from jax.experimental import pallas as pl
from jax.experimental.pallas import tpu as pltpu
from jax.sharding import PartitionSpec as P

MESH = pl.DeviceIdType.MESH
BF, F32 = jnp.bfloat16, jnp.float32
ITERS = 2
UNIT = 512
HALF = 688
DEEP = 1024


def dot(a, b, ca, cb):
    return lax.dot_general(a, b, (((ca,), (cb,)), ((), ())), preferred_element_type=F32)


def exact(a, b, ca, cb):
    return lax.dot_general(
        a, b, (((ca,), (cb,)), ((), ())), precision=lax.Precision.HIGHEST, preferred_element_type=F32
    )


def split(v):
    hi = v.astype(BF)
    rest = v - hi.astype(F32)
    mid = rest.astype(BF)
    low = (rest - mid.astype(F32)).astype(BF)
    return jnp.concatenate([hi, mid, low], axis=0)


def fold(v):
    r = v.shape[0] // 3
    return v[:r] + (v[r : 2 * r] + v[2 * r :])


def inverse_factor(gram):
    r = gram.shape[0]
    row = lax.broadcasted_iota(jnp.int32, (r, 2 * r), 0)
    col = lax.broadcasted_iota(jnp.int32, (r, 2 * r), 1)
    eye = (row == col)[:, :r].astype(F32)
    a = jnp.concatenate([gram, eye], axis=1)
    for j in range(r):
        factor = a[:, j : j + 1] / a[j : j + 1, j : j + 1]
        a = a - jnp.where(row > j, factor, 0.0) * a[j : j + 1, :]
    pivots = jnp.sum(jnp.where(row == col, a, 0.0), axis=1, keepdims=True)
    return a[:, r:] * lax.rsqrt(pivots)


def factors_kernel(
    x_h, y_h, e_h, q0_h, left_o, right_o, qt_o, x, y, e,
    et, q0, qs, ps, xq, pacc, wacc, sacc, linv,
    pout, pin, pown, slots, pt, wloc, wrx, wz, wfull,
    in_sem, near_sem, far_sem, cx_s, cx_r, rs_s, rs_r, ag_s, ag_r, fw_s, fw_r, wx_s, wx_r, wz_s, wz_r, wf_s, wf_r,
):
    dp, mp = lax.axis_index("dp"), lax.axis_index("mp")
    z, c = lax.div(dp, 2), lax.rem(dp, 2)
    px, py = lax.div(mp, 4), lax.rem(mp, 4)
    o = 1 - c
    partner = (z * 2 + o, mp)
    at_x = [lax.rem(px + k, 4) for k in range(4)]
    at_y = [lax.rem(py + k, 4) for k in range(4)]
    at_z = [lax.rem(z + k, 4) for k in range(4)]
    far_first = (2, 1, 3, 0)
    others = [(dx, dy, dz) for dx in far_first for dy in far_first for dz in far_first][:-1]

    def chip(dx, dy, dz):
        return (at_z[dz] * 2 + c, at_x[dx] * 4 + at_y[dy])

    def cols(half, u):
        return pl.ds(pl.multiple_of(half * 2048 + u * UNIT, UNIT), UNIT)

    def deep(k):
        return pl.ds(pl.multiple_of(k * DEEP, DEEP), DEEP)

    def half_rows(h):
        return pl.ds(pl.multiple_of(h * HALF, 16), HALF)

    def remote(src, dst, ss, rs, to):
        return pltpu.make_async_remote_copy(src, dst, ss, rs, device_id=to, device_id_type=MESH)

    def arrived(ref, sem):
        pltpu.make_async_copy(ref, ref, sem).wait()

    barrier = pltpu.get_barrier_semaphore()
    for peer in others:
        pl.semaphore_signal(barrier, inc=1, device_id=chip(*peer), device_id_type=MESH)
    pl.semaphore_signal(barrier, inc=1, device_id=partner, device_id_type=MESH)

    loads = [
        pltpu.make_async_copy(q0_h, q0, in_sem.at[0]),
        pltpu.make_async_copy(y_h, y, in_sem.at[1]),
        pltpu.make_async_copy(x_h, x, in_sem.at[2]),
    ]

    def own_load(k):
        at = (half_rows(c), deep(k))
        return pltpu.make_async_copy(e_h.at[0, at[0], at[1]], e.at[at[0], at[1]], near_sem.at[k])

    def other_load(k):
        at = (half_rows(o), cols(c if k >= 4 else o, at_x[far_first[k % 4]]))
        return pltpu.make_async_copy(e_h.at[0, at[0], at[1]], e.at[at[0], at[1]], far_sem.at[k])

    loads[0].start()
    own_load(0).start()
    loads[1].start()
    for k in range(1, 4):
        own_load(k).start()
    loads[2].start()
    for k in range(8):
        other_load(k).start()

    loads[0].wait()
    for h in range(2):
        qs[h] = split(q0[:, h * HALF : h * HALF + HALF])

    def iteration(it, carry):
        for k in range(4):
            @pl.when(it == 0)
            def _():
                own_load(k).wait()

            pacc[:, deep(k)] = fold(dot(qs[c], e[half_rows(c), deep(k)], 1, 0))

        @pl.when(it > 0)
        def _():
            arrived(wfull.at[it - 1, o], wf_r.at[it - 1])
            qs[o] = split(exact(0.125 * linv[...], wfull[it - 1, o], 1, 0))

        @pl.when(it == 0)
        def _():
            loads[1].wait()
            loads[2].wait()
            pl.semaphore_wait(barrier, 64)

        xq[...] = split(fold(dot(qs[0], y[:HALF], 1, 0) + dot(qs[1], y[HALF:], 1, 0)))

        def term(k, half, u):
            @pl.when(it == 0)
            def _():
                other_load(k).wait()

            at = cols(half, u)
            return pacc[:, at] + fold(dot(qs[o], e[half_rows(o), at], 1, 0) + dot(xq[...], x[:, at], 1, 0))

        for i, dx in enumerate(far_first):
            v = term(i, o, at_x[dx])
            for t in range(4):
                pout[it, i, t] = v[:, 128 * t : 128 * t + 128]
            remote(pout.at[it, i], pin.at[it, i], cx_s.at[it], cx_r.at[it, i], partner).start()

        for i, dx in enumerate(far_first):
            u = at_x[dx]
            v = term(i + 4, c, u)
            arrived(pin.at[it, i], cx_r.at[it, i])
            for t in range(4):
                pown[it, u, t] = v[:, 128 * t : 128 * t + 128] + pin[it, i, t]
            for dy in far_first:
                for dz in far_first:
                    if dx or dy or dz:
                        src = pown.at[it, u, at_y[dy], pl.ds(pl.multiple_of(at_z[dz] * 8, 8), 8), :]
                        slot = slots.at[it, dx * 16 + dy * 4 + dz]
                        remote(src, slot, rs_s.at[it], rs_r.at[it], chip(dx, dy, dz)).start()

        @pl.when(it == 0)
        def _():
            def flip(k, carry):
                for h in range(2):
                    et[h, cols(0, k), :] = jnp.transpose(e[half_rows(h), cols(0, k)])
                return carry

            lax.fori_loop(0, 8, flip, 0)

        mine = pl.ds(pl.multiple_of(z * 8, 8), 8)
        slots[it, 0] = pown[it, px, py, mine, :]
        arrived(slots.at[it, pl.ds(1, 63)], rs_r.at[it])
        pt[it, c, px * 4 + py, mine, :] = jnp.sum(slots[it], axis=0)
        tile = pt.at[it, c, px * 4 + py, mine, :]
        for peer in others:
            remote(tile, tile, ag_s.at[it], ag_r.at[it], chip(*peer)).start()
        arrived(slots.at[it, pl.ds(1, 63)], ag_r.at[it])
        for g in range(2):
            block = pt.at[it, c, pl.ds(8 * g, 8)]
            remote(block, block, fw_s.at[it], fw_r.at[it, g], partner).start()

        def piece(half, g):
            return split(jnp.concatenate([pt[it, half, 8 * g + t] for t in range(8)], axis=1))

        for g in range(2):
            at = deep(2 * c + g)
            p = piece(c, g)
            for h in range(2):
                w = dot(p, et[h, at, :], 1, 0)
                wacc[h] = w if g == 0 else wacc[h] + w
            w = dot(p, x[:, at], 1, 1)
            sacc[...] = w if g == 0 else sacc[...] + w
        for g in range(2):
            arrived(pt.at[it, o, pl.ds(8 * g, 8)], fw_r.at[it, g])
            p = piece(o, g)
            ps[:, g * DEEP : g * DEEP + DEEP] = p
            sacc[...] += dot(p, x[:, deep(2 * o + g)], 1, 1)
        s = split(fold(sacc[...]))

        def finish(h):
            at = pl.ds(pl.multiple_of(o * 2048, 2048), 2048)
            return fold(wacc[h] + dot(ps[...], et[h, at, :], 1, 0) + dot(s, y[half_rows(h), :], 1, 1))

        wloc[it] = finish(o)
        remote(wloc.at[it], wrx.at[it], wx_s.at[it], wx_r.at[it], partner).start()
        w = finish(c)
        arrived(wrx.at[it], wx_r.at[it])
        wz[it, z] = w + wrx[it]
        for dz in (2, 1, 3):
            remote(wz.at[it, z], wz.at[it, z], wz_s.at[it], wz_r.at[it, dz], chip(0, 0, dz)).start()

        def add_gram(k, total):
            p = split(jnp.concatenate([pt[it, k // 2, (k % 2) * 8 + t] for t in range(8)], axis=1))
            return total + dot(p, p, 1, 1)

        gram = fold(lax.fori_loop(0, 4, add_gram, jnp.zeros((96, 96), F32)))
        gram = gram[:, :32] + (gram[:, 32:64] + gram[:, 64:])
        linv[...] = inverse_factor(gram)

        @pl.when(it == ITERS - 1)
        def _():
            def write_left(k, carry):
                p = jnp.concatenate([pt[it, k // 4, (k % 4) * 4 + t] for t in range(4)], axis=1)
                p = split(-exact(linv[...], p, 1, 0))
                left_o[:, cols(0, k)] = jnp.concatenate([p[:32], p[:32], p[32:64], p[32:64]], axis=0)
                return carry

            lax.fori_loop(0, 8, write_left, 0)

        for dz in (1, 3, 2):
            arrived(wz.at[it, at_z[4 - dz]], wz_r.at[it, dz])
        wfull[it, c] = ((wz[it, 0] + wz[it, 1]) + wz[it, 2]) + wz[it, 3]
        remote(wfull.at[it, c], wfull.at[it, c], wf_s.at[it], wf_r.at[it], partner).start()
        qs[c] = split(exact(0.125 * linv[...], wfull[it, c], 1, 0))
        return carry

    lax.fori_loop(0, ITERS, iteration, 0)
    last = ITERS - 1
    arrived(wfull.at[last, o], wf_r.at[last])
    for h in range(2):
        q = exact(0.125 * linv[...], wfull[last, h], 1, 0)
        qt_o[:, h * HALF : h * HALF + HALF] = q
        q = split(q)[:64].astype(F32)
        right_o[h * HALF : h * HALF + HALF] = jnp.transpose(jnp.concatenate([q, q], axis=0)).astype(BF)

    for it in range(ITERS):
        arrived(pout.at[it], cx_s.at[it])
        arrived(slots.at[it, pl.ds(1, 63)], rs_s.at[it])
        arrived(slots.at[it, pl.ds(1, 63)], ag_s.at[it])
        arrived(pt.at[it, c], fw_s.at[it])
        arrived(wrx.at[it], wx_s.at[it])
        arrived(wz.at[it, pl.ds(0, 3)], wz_s.at[it])
        arrived(wfull.at[it, c], wf_s.at[it])


def error_kernel(e, x, left, y, right, qt, out, q_out, stage, sem):
    k = jnp.concatenate([y[...], right[...]], axis=1)
    q_out[...] = qt[...]

    def write(i):
        at = pl.ds(pl.multiple_of(i * DEEP, DEEP), DEEP)
        return pltpu.make_async_copy(stage.at[i % 2], out.at[0, :, at], sem.at[i % 2])

    for i in range(4):
        if i >= 2:
            write(i - 2).wait()
        at = pl.ds(i * DEEP, DEEP)
        r = jnp.concatenate([x[:, at], left[:, at]], axis=0)
        stage[i % 2] = (e[:, at].astype(F32) + dot(k, r, 1, 0)).astype(BF)
        write(i).start()
    write(2).wait()
    write(3).wait()


def local(inputs, grad_out, error, q_prev):
    grad_out, q_prev, error = grad_out.T, q_prev.T, jnp.swapaxes(error, 1, 2)
    tokens, dw = inputs.shape
    rank, ff = q_prev.shape
    vmem = pl.BlockSpec(memory_space=pltpu.VMEM)
    anywhere = pl.BlockSpec(memory_space=pl.ANY)
    dma = pltpu.SemaphoreType.DMA
    left, right, qt, x, y, e = pl.pallas_call(
        factors_kernel,
        out_shape=(
            jax.ShapeDtypeStruct((4 * rank, dw), BF),
            jax.ShapeDtypeStruct((ff, 4 * rank), BF),
            jax.ShapeDtypeStruct((rank, ff), F32),
            jax.ShapeDtypeStruct((tokens, dw), BF),
            jax.ShapeDtypeStruct((ff, tokens), BF),
            jax.ShapeDtypeStruct((ff, dw), BF),
        ),
        in_specs=[anywhere] * 4,
        out_specs=(vmem,) * 6,
        scratch_shapes=[
            pltpu.VMEM((2, dw, HALF), BF),
            pltpu.VMEM((rank, ff), F32),
            pltpu.VMEM((2, 3 * rank, HALF), BF),
            pltpu.VMEM((3 * rank, 2 * DEEP), BF),
            pltpu.VMEM((3 * rank, tokens), BF),
            pltpu.VMEM((rank, dw), F32),
            pltpu.VMEM((2, 3 * rank, HALF), F32),
            pltpu.VMEM((3 * rank, tokens), F32),
            pltpu.VMEM((rank, rank), F32),
            pltpu.VMEM((2, 4, 4, rank, 128), F32),
            pltpu.VMEM((2, 4, 4, rank, 128), F32),
            pltpu.VMEM((2, 4, 4, rank, 128), F32),
            pltpu.VMEM((2, 64, 8, 128), F32),
            pltpu.VMEM((2, 2, 16, rank, 128), F32),
            pltpu.VMEM((2, rank, HALF), F32),
            pltpu.VMEM((2, rank, HALF), F32),
            pltpu.VMEM((2, 4, rank, HALF), F32),
            pltpu.VMEM((2, 2, rank, HALF), F32),
            dma((3,)), dma((4,)), dma((8,)),
            dma((2,)), dma((2, 4)),
            dma((2,)), dma((2,)),
            dma((2,)), dma((2,)),
            dma((2,)), dma((2, 2)),
            dma((2,)), dma((2,)),
            dma((2,)), dma((2, 4)),
            dma((2,)), dma((2,)),
        ],
        compiler_params=pltpu.CompilerParams(
            collective_id=0, has_side_effects=True, vmem_limit_bytes=28 * 2**20
        ),
        name="power_iterations",
    )(*[pltpu.with_memory_space_constraint(v, pltpu.HBM) for v in (inputs, grad_out, error, q_prev)])
    new_error, q_new = pl.pallas_call(
        error_kernel,
        out_shape=(jax.ShapeDtypeStruct(error.shape, BF), jax.ShapeDtypeStruct((rank, ff), F32)),
        in_specs=[vmem] * 6,
        out_specs=(anywhere, vmem),
        scratch_shapes=[pltpu.VMEM((2, ff, DEEP), BF), dma((2,))],
        compiler_params=pltpu.CompilerParams(vmem_limit_bytes=24 * 2**20),
        name="new_error",
    )(e, x, left, y, right, qt)
    return jnp.swapaxes(new_error, 1, 2), q_new.T


def solution(mesh):
    placed = (P("dp", None), P("dp", "mp"), P("dp", None, "mp"), P("mp", None))
    return jax.shard_map(
        local,
        mesh=mesh,
        in_specs=placed,
        out_specs=(P("dp", None, "mp"), P("mp", None)),
        check_vma=False,
    )
```

```python
import jax
import jax.numpy as jnp
from jax import lax
from jax.experimental import pallas as pl
from jax.experimental.pallas import tpu as pltpu
from jax.sharding import PartitionSpec as P

MESH = pl.DeviceIdType.MESH
BF, F32 = jnp.bfloat16, jnp.float32
ITERS = 2
UNIT = 512
HALF = 688
PARTS = ((0, 256), (256, 256), (512, 176))
DEEP = 1024


def dot(a, b, ca, cb):
    return lax.dot_general(a, b, (((ca,), (cb,)), ((), ())), preferred_element_type=F32)


def exact(a, b, ca, cb):
    return lax.dot_general(
        a, b, (((ca,), (cb,)), ((), ())), precision=lax.Precision.HIGHEST, preferred_element_type=F32
    )


def split(v):
    hi = v.astype(BF)
    rest = v - hi.astype(F32)
    mid = rest.astype(BF)
    low = (rest - mid.astype(F32)).astype(BF)
    return jnp.concatenate([hi, mid, low], axis=0)


def fold(v):
    r = v.shape[0] // 3
    return v[:r] + (v[r : 2 * r] + v[2 * r :])


def inverse_factor(gram):
    r = gram.shape[0]
    row = lax.broadcasted_iota(jnp.int32, (r, 2 * r), 0)
    col = lax.broadcasted_iota(jnp.int32, (r, 2 * r), 1)
    eye = (row == col)[:, :r].astype(F32)
    a = jnp.concatenate([gram, eye], axis=1)
    for j in range(r):
        factor = a[:, j : j + 1] / a[j : j + 1, j : j + 1]
        a = a - jnp.where(row > j, factor, 0.0) * a[j : j + 1, :]
    pivots = jnp.sum(jnp.where(row == col, a, 0.0), axis=1, keepdims=True)
    return a[:, r:] * lax.rsqrt(pivots)


def factors_kernel(
    x_h, y_h, e_h, q0_h, left_o, right_o, qt_o, base_o,
    x, y, e, et, q0, qs, ps, xq, tacc, pacc, wacc, sacc, linv,
    pout, pin, pown, slots, pt, wloc, wrx, wz, wfull,
    in_sem, near_sem, far_sem, cx_s, cx_r, rs_s, rs_r, ag_s, ag_r, fw_s, fw_r, wx_s, wx_r, wz_s, wz_r, wf_s, wf_r,
):
    dp, mp = lax.axis_index("dp"), lax.axis_index("mp")
    z, c = lax.div(dp, 2), lax.rem(dp, 2)
    px, py = lax.div(mp, 4), lax.rem(mp, 4)
    o = 1 - c
    partner = (z * 2 + o, mp)
    at_x = [lax.rem(px + k, 4) for k in range(4)]
    at_y = [lax.rem(py + k, 4) for k in range(4)]
    at_z = [lax.rem(z + k, 4) for k in range(4)]
    far_first = (2, 1, 3, 0)
    others = [(dx, dy, dz) for dx in far_first for dy in far_first for dz in far_first][:-1]

    def chip(dx, dy, dz):
        return (at_z[dz] * 2 + c, at_x[dx] * 4 + at_y[dy])

    def cols(half, u):
        return pl.ds(pl.multiple_of(half * 2048 + u * UNIT, UNIT), UNIT)

    def deep(k):
        return pl.ds(pl.multiple_of(k * DEEP, DEEP), DEEP)

    def half_rows(h):
        return pl.ds(pl.multiple_of(h * HALF, 16), HALF)

    def part_rows(h, k):
        first, width = PARTS[k]
        return pl.ds(pl.multiple_of(h * HALF + first, 16), width)

    def lanes(k):
        return pl.ds(*PARTS[k])

    def remote(src, dst, ss, rs, to):
        return pltpu.make_async_remote_copy(src, dst, ss, rs, device_id=to, device_id_type=MESH)

    def arrived(ref, sem):
        pltpu.make_async_copy(ref, ref, sem).wait()

    barrier = pltpu.get_barrier_semaphore()
    for peer in others:
        pl.semaphore_signal(barrier, inc=1, device_id=chip(*peer), device_id_type=MESH)
    pl.semaphore_signal(barrier, inc=1, device_id=partner, device_id_type=MESH)

    loads = [
        pltpu.make_async_copy(q0_h, q0, in_sem.at[0]),
        pltpu.make_async_copy(y_h, y, in_sem.at[1]),
        pltpu.make_async_copy(x_h, x, in_sem.at[2]),
    ]

    def own_load(k):
        at = part_rows(c, k)
        return pltpu.make_async_copy(e_h.at[0, at, :], e.at[at, :], near_sem.at[k])

    def other_load(k):
        at = (half_rows(o), cols(c if k >= 4 else o, at_x[far_first[k % 4]]))
        return pltpu.make_async_copy(e_h.at[0, at[0], at[1]], e.at[at[0], at[1]], far_sem.at[k])

    loads[0].start()
    own_load(0).start()
    loads[1].start()
    for k in range(1, 3):
        own_load(k).start()
    loads[2].start()
    for k in range(8):
        other_load(k).start()

    wz[...] = jnp.zeros_like(wz)
    wloc[...] = jnp.zeros_like(wloc)
    loads[0].wait()
    for h in range(2):
        qs[h] = split(q0[:, h * HALF : h * HALF + HALF])

    def enter(k):
        q, at = qs[c, :, lanes(k)], part_rows(c, k)
        t = dot(q, y[at, :], 1, 0)
        tacc[...] = t if k == 0 else tacc[...] + t
        for j in range(2):
            to = pl.ds(j * 2048, 2048)
            v = fold(dot(q, e[at, to], 1, 0))
            pacc[:, to] = v if k == 0 else pacc[:, to] + v

    loads[1].wait()
    for k in range(3):
        own_load(k).wait()
        enter(k)
    loads[2].wait()
    pl.semaphore_wait(barrier, 64)

    def iteration(it, carry):
        @pl.when(it > 0)
        def _():
            for k in range(3):
                arrived(wfull.at[it - 1, o, k], wf_r.at[it - 1, k])
                qs[o, :, lanes(k)] = split(exact(0.125 * linv[...], wfull[it - 1, o, k], 1, 0))[:, : PARTS[k][1]]

        xq[...] = split(fold(tacc[...] + dot(qs[o], y[half_rows(o), :], 1, 0)))

        def term(k, half, u):
            @pl.when(it == 0)
            def _():
                other_load(k).wait()

            at = cols(half, u)
            return pacc[:, at] + fold(dot(qs[o], e[half_rows(o), at], 1, 0) + dot(xq[...], x[:, at], 1, 0))

        for i, dx in enumerate(far_first):
            v = term(i, o, at_x[dx])
            for t in range(4):
                pout[it, i, t] = v[:, 128 * t : 128 * t + 128]
            remote(pout.at[it, i], pin.at[it, i], cx_s.at[it], cx_r.at[it, i], partner).start()

        for i, dx in enumerate(far_first):
            u = at_x[dx]
            v = term(i + 4, c, u)
            arrived(pin.at[it, i], cx_r.at[it, i])
            for t in range(4):
                pown[it, u, t] = v[:, 128 * t : 128 * t + 128] + pin[it, i, t]
            for dy in far_first:
                for dz in far_first:
                    if dx or dy or dz:
                        src = pown.at[it, u, at_y[dy], pl.ds(pl.multiple_of(at_z[dz] * 8, 8), 8), :]
                        slot = slots.at[it, dx * 16 + dy * 4 + dz]
                        remote(src, slot, rs_s.at[it], rs_r.at[it], chip(dx, dy, dz)).start()

        @pl.when(it == 0)
        def _():
            def flip(k, carry):
                for h in range(2):
                    et[h, cols(0, k), :] = jnp.transpose(e[half_rows(h), cols(0, k)])
                return carry

            lax.fori_loop(0, 8, flip, 0)

        mine = pl.ds(pl.multiple_of(z * 8, 8), 8)
        slots[it, 0] = pown[it, px, py, mine, :]
        arrived(slots.at[it, pl.ds(1, 63)], rs_r.at[it])
        pt[it, c, px * 4 + py, mine, :] = jnp.sum(slots[it], axis=0)
        tile = pt.at[it, c, px * 4 + py, mine, :]
        for peer in others:
            remote(tile, tile, ag_s.at[it], ag_r.at[it], chip(*peer)).start()

        def merge(k, carry):
            at = cols(it, k)
            base_o[:, at] = dot(y[...], x[:, at], 1, 0) + e[:, at].astype(F32)
            return carry

        lax.fori_loop(0, 4, merge, 0)
        arrived(slots.at[it, pl.ds(1, 63)], ag_r.at[it])
        for g in range(2):
            block = pt.at[it, c, pl.ds(8 * g, 8)]
            remote(block, block, fw_s.at[it], fw_r.at[it, g], partner).start()

        def piece(half, g):
            return split(jnp.concatenate([pt[it, half, 8 * g + t] for t in range(8)], axis=1))

        for g in range(2):
            at = deep(2 * c + g)
            p = piece(c, g)
            for h in range(2):
                w = dot(p, et[h, at, :], 1, 0)
                wacc[h] = w if g == 0 else wacc[h] + w
            w = dot(p, x[:, at], 1, 1)
            sacc[...] = w if g == 0 else sacc[...] + w
        for g in range(2):
            arrived(pt.at[it, o, pl.ds(8 * g, 8)], fw_r.at[it, g])
            p = piece(o, g)
            ps[:, g * DEEP : g * DEEP + DEEP] = p
            sacc[...] += dot(p, x[:, deep(2 * o + g)], 1, 1)
        s = split(fold(sacc[...]))

        def finish(h, k):
            at = pl.ds(pl.multiple_of(o * 2048, 2048), 2048)
            w = wacc[h, :, lanes(k)] + dot(ps[...], et[h, at, lanes(k)], 1, 0)
            return fold(w + dot(s, y[part_rows(h, k), :], 1, 1))

        for k in range(3):
            wloc[it, k, :, : PARTS[k][1]] = finish(o, k)
            remote(wloc.at[it, k], wrx.at[it, k], wx_s.at[it], wx_r.at[it, k], partner).start()
        for k in range(3):
            w = finish(c, k)
            arrived(wrx.at[it, k], wx_r.at[it, k])
            wz[it, k, z, :, : PARTS[k][1]] = w + wrx[it, k, :, : PARTS[k][1]]
            mine_z = wz.at[it, k, z]
            for dz in (2, 1, 3):
                remote(mine_z, mine_z, wz_s.at[it], wz_r.at[it, k, dz], chip(0, 0, dz)).start()

        def add_gram(k, total):
            p = split(jnp.concatenate([pt[it, k // 2, (k % 2) * 8 + t] for t in range(8)], axis=1))
            return total + dot(p, p, 1, 1)

        gram = fold(lax.fori_loop(0, 4, add_gram, jnp.zeros((96, 96), F32)))
        gram = gram[:, :32] + (gram[:, 32:64] + gram[:, 64:])
        linv[...] = inverse_factor(gram)

        @pl.when(it == ITERS - 1)
        def _():
            def write_left(k, carry):
                p = jnp.concatenate([pt[it, k // 4, (k % 4) * 4 + t] for t in range(4)], axis=1)
                p = split(-exact(linv[...], p, 1, 0))
                left_o[:, cols(0, k)] = jnp.concatenate([p[:32], p[:32], p[32:64], p[32:64]], axis=0)
                return carry

            lax.fori_loop(0, 8, write_left, 0)

        for k in range(3):
            for dz in (1, 3, 2):
                arrived(wz.at[it, k, at_z[4 - dz]], wz_r.at[it, k, dz])
            total = ((wz[it, k, 0] + wz[it, k, 1]) + wz[it, k, 2]) + wz[it, k, 3]
            wfull[it, c, k] = total
            block = wfull.at[it, c, k]
            remote(block, block, wf_s.at[it], wf_r.at[it, k], partner).start()
            qs[c, :, lanes(k)] = split(exact(0.125 * linv[...], total, 1, 0))[:, : PARTS[k][1]]

            @pl.when(it < ITERS - 1)
            def _():
                enter(k)

        return carry

    lax.fori_loop(0, ITERS, iteration, 0)
    last = ITERS - 1
    for k in range(3):
        arrived(wfull.at[last, o, k], wf_r.at[last, k])
    for h in range(2):
        for k in range(3):
            q = exact(0.125 * linv[...], wfull[last, h, k], 1, 0)
            first, width = h * HALF + PARTS[k][0], PARTS[k][1]
            qt_o[:, first : first + width] = q[:, :width]
            q = split(q)[:64].astype(F32)
            q = jnp.transpose(jnp.concatenate([q, q], axis=0))
            right_o[first : first + width] = q[:width].astype(BF)

    for it in range(ITERS):
        arrived(pout.at[it], cx_s.at[it])
        arrived(slots.at[it, pl.ds(1, 63)], rs_s.at[it])
        arrived(slots.at[it, pl.ds(1, 63)], ag_s.at[it])
        arrived(pt.at[it, c], fw_s.at[it])
        arrived(wrx.at[it], wx_s.at[it])
        arrived(wz.at[it, pl.ds(0, 3), pl.ds(0, 3)], wz_s.at[it])
        arrived(wfull.at[it, c], wf_s.at[it])


def error_kernel(base, left, right, qt, out, q_out, stage, sem):
    q_out[...] = qt[...]

    def write(i):
        at = pl.ds(pl.multiple_of(i * DEEP, DEEP), DEEP)
        return pltpu.make_async_copy(stage.at[i % 2], out.at[0, :, at], sem.at[i % 2])

    for i in range(4):
        if i >= 2:
            write(i - 2).wait()
        at = pl.ds(i * DEEP, DEEP)
        stage[i % 2] = (base[:, at] + dot(right[...], left[:, at], 1, 0)).astype(BF)
        write(i).start()
    write(2).wait()
    write(3).wait()


def local(inputs, grad_out, error, q_prev):
    grad_out, q_prev, error = grad_out.T, q_prev.T, jnp.swapaxes(error, 1, 2)
    tokens, dw = inputs.shape
    rank, ff = q_prev.shape
    vmem = pl.BlockSpec(memory_space=pltpu.VMEM)
    anywhere = pl.BlockSpec(memory_space=pl.ANY)
    dma = pltpu.SemaphoreType.DMA
    left, right, qt, base = pl.pallas_call(
        factors_kernel,
        out_shape=(
            pltpu.VMEM((4 * rank, dw), BF),
            pltpu.VMEM((ff, 4 * rank), BF),
            pltpu.VMEM((rank, ff), F32),
            pltpu.VMEM((ff, dw), F32),
        ),
        in_specs=[anywhere] * 4,
        out_specs=(vmem,) * 4,
        scratch_shapes=[
            pltpu.VMEM((tokens, dw), BF),
            pltpu.VMEM((ff, tokens), BF),
            pltpu.VMEM((ff, dw), BF),
            pltpu.VMEM((2, dw, HALF), BF),
            pltpu.VMEM((rank, ff), F32),
            pltpu.VMEM((2, 3 * rank, HALF), BF),
            pltpu.VMEM((3 * rank, 2 * DEEP), BF),
            pltpu.VMEM((3 * rank, tokens), BF),
            pltpu.VMEM((3 * rank, tokens), F32),
            pltpu.VMEM((rank, dw), F32),
            pltpu.VMEM((2, 3 * rank, HALF), F32),
            pltpu.VMEM((3 * rank, tokens), F32),
            pltpu.VMEM((rank, rank), F32),
            pltpu.VMEM((2, 4, 4, rank, 128), F32),
            pltpu.VMEM((2, 4, 4, rank, 128), F32),
            pltpu.VMEM((2, 4, 4, rank, 128), F32),
            pltpu.VMEM((2, 64, 8, 128), F32),
            pltpu.VMEM((2, 2, 16, rank, 128), F32),
            pltpu.VMEM((2, 3, rank, 256), F32),
            pltpu.VMEM((2, 3, rank, 256), F32),
            pltpu.VMEM((2, 3, 4, rank, 256), F32),
            pltpu.VMEM((2, 2, 3, rank, 256), F32),
            dma((3,)), dma((3,)), dma((8,)),
            dma((2,)), dma((2, 4)),
            dma((2,)), dma((2,)),
            dma((2,)), dma((2,)),
            dma((2,)), dma((2, 2)),
            dma((2,)), dma((2, 3)),
            dma((2,)), dma((2, 3, 4)),
            dma((2,)), dma((2, 3)),
        ],
        compiler_params=pltpu.CompilerParams(
            collective_id=0, has_side_effects=True, vmem_limit_bytes=36 * 2**20
        ),
        name="power_iterations",
    )(*[pltpu.with_memory_space_constraint(v, pltpu.HBM) for v in (inputs, grad_out, error, q_prev)])
    new_error, q_new = pl.pallas_call(
        error_kernel,
        out_shape=(jax.ShapeDtypeStruct(error.shape, BF), jax.ShapeDtypeStruct((rank, ff), F32)),
        in_specs=[vmem] * 4,
        out_specs=(anywhere, vmem),
        scratch_shapes=[pltpu.VMEM((2, ff, DEEP), BF), dma((2,))],
        compiler_params=pltpu.CompilerParams(vmem_limit_bytes=16 * 2**20),
        name="new_error",
    )(base, left, right, qt)
    return jnp.swapaxes(new_error, 1, 2), q_new.T


def solution(mesh):
    placed = (P("dp", None), P("dp", "mp"), P("dp", None, "mp"), P("mp", None))
    return jax.shard_map(
        local,
        mesh=mesh,
        in_specs=placed,
        out_specs=(P("dp", None, "mp"), P("mp", None)),
        check_vma=False,
    )
```

```python
import jax
import jax.numpy as jnp
from jax import lax
from jax.experimental import pallas as pl
from jax.experimental.pallas import tpu as pltpu
from jax.sharding import PartitionSpec as P

MESH = pl.DeviceIdType.MESH
BF, F32 = jnp.bfloat16, jnp.float32
ITERS = 2
UNIT = 512
HALF = 688
PARTS = ((0, 256), (256, 256), (512, 176))
DEEP = 1024


def dot(a, b, ca, cb):
    return lax.dot_general(a, b, (((ca,), (cb,)), ((), ())), preferred_element_type=F32)


def exact(a, b, ca, cb):
    return lax.dot_general(
        a, b, (((ca,), (cb,)), ((), ())), precision=lax.Precision.HIGHEST, preferred_element_type=F32
    )


def split(v):
    hi = v.astype(BF)
    rest = v - hi.astype(F32)
    mid = rest.astype(BF)
    low = (rest - mid.astype(F32)).astype(BF)
    return jnp.concatenate([hi, mid, low], axis=0)


def fold(v):
    r = v.shape[0] // 3
    return v[:r] + (v[r : 2 * r] + v[2 * r :])


def inverse_factor(gram):
    r = gram.shape[0]
    row = lax.broadcasted_iota(jnp.int32, (r, 2 * r), 0)
    col = lax.broadcasted_iota(jnp.int32, (r, 2 * r), 1)
    eye = (row == col)[:, :r].astype(F32)
    a = jnp.concatenate([gram, eye], axis=1)
    for j in range(r):
        factor = a[:, j : j + 1] / a[j : j + 1, j : j + 1]
        a = a - jnp.where(row > j, factor, 0.0) * a[j : j + 1, :]
    pivots = jnp.sum(jnp.where(row == col, a, 0.0), axis=1, keepdims=True)
    return a[:, r:] * lax.rsqrt(pivots)


def factors_kernel(
    x_h, y_h, e_h, q0_h, left_o, right_o, qt_o, base_o,
    x, y, e, et, q0, qs, ps, xq, tacc, pacc, wacc, sacc, linv,
    pout, pin, pown, slots, pt, wloc, wrx, wz, wfull,
    in_sem, e_sem, cx_s, cx_r, rs_s, rs_r, ag_s, ag_r, fw_s, fw_r, wx_s, wx_r, wz_s, wz_r, wf_s, wf_r,
):
    dp, mp = lax.axis_index("dp"), lax.axis_index("mp")
    z, c = lax.div(dp, 2), lax.rem(dp, 2)
    px, py = lax.div(mp, 4), lax.rem(mp, 4)
    o = 1 - c
    partner = (z * 2 + o, mp)
    at_x = [lax.rem(px + k, 4) for k in range(4)]
    at_y = [lax.rem(py + k, 4) for k in range(4)]
    at_z = [lax.rem(z + k, 4) for k in range(4)]
    far_first = (2, 1, 3, 0)
    odd = lax.rem(px, 2)
    pairs = (lax.div(at_x[2], 2), 1 - lax.div(at_x[2], 2))
    pair_offsets = ((2, 3 - 2 * odd), (1 + 2 * odd, 0))
    others = [(dx, dy, dz) for dx in far_first for dy in far_first for dz in far_first][:-1]
    others.sort(key=lambda peer: -sum(min(k, 4 - k) for k in peer))

    def chip(dx, dy, dz):
        return (at_z[dz] * 2 + c, at_x[dx] * 4 + at_y[dy])

    def cols(half, u):
        return pl.ds(pl.multiple_of(half * 2048 + u * UNIT, UNIT), UNIT)

    def deep(k):
        return pl.ds(pl.multiple_of(k * DEEP, DEEP), DEEP)

    def half_rows(h):
        return pl.ds(pl.multiple_of(h * HALF, 16), HALF)

    def part_rows(h, k):
        first, width = PARTS[k]
        return pl.ds(pl.multiple_of(h * HALF + first, 16), width)

    def lanes(k):
        return pl.ds(*PARTS[k])

    def remote(src, dst, ss, rs, to):
        return pltpu.make_async_remote_copy(src, dst, ss, rs, device_id=to, device_id_type=MESH)

    def arrived(ref, sem):
        pltpu.make_async_copy(ref, ref, sem).wait()

    barrier = pltpu.get_barrier_semaphore()
    for peer in others:
        pl.semaphore_signal(barrier, inc=1, device_id=chip(*peer), device_id_type=MESH)
    pl.semaphore_signal(barrier, inc=1, device_id=partner, device_id_type=MESH)

    loads = [
        pltpu.make_async_copy(q0_h, q0, in_sem.at[0]),
        pltpu.make_async_copy(y_h, y, in_sem.at[1]),
        pltpu.make_async_copy(x_h, x, in_sem.at[2]),
    ]

    order = ((c, 0), (c, 1), (c, 2), (o, 0), (o, 1), (o, 2))

    def part_load(n):
        at = part_rows(*order[n])
        return pltpu.make_async_copy(e_h.at[0, at, :], e.at[at, :], e_sem.at[n])

    loads[0].start()
    part_load(0).start()
    loads[1].start()
    for n in range(1, 5):
        part_load(n).start()
    loads[2].start()
    part_load(5).start()

    wz[...] = jnp.zeros_like(wz)
    wloc[...] = jnp.zeros_like(wloc)
    loads[0].wait()
    for h in range(2):
        qs[h] = split(q0[:, h * HALF : h * HALF + HALF])

    def enter(h, k, first=False):
        q, at = qs[h, :, lanes(k)], part_rows(h, k)
        t = dot(q, y[at, :], 1, 0)
        tacc[...] = t if first else tacc[...] + t
        for j in range(2):
            to = pl.ds(j * 2048, 2048)
            v = fold(dot(q, e[at, to], 1, 0))
            pacc[:, to] = v if first else pacc[:, to] + v

    def take(it, h, k):
        qs[h, :, lanes(k)] = split(exact(0.125 * linv[...], wfull[it, h, k], 1, 0))[:, : PARTS[k][1]]

    def take_partner(it, k):
        arrived(wfull.at[it, o, k], wf_r.at[it, k])
        take(it, o, k)

    loads[1].wait()
    for n in range(5):
        part_load(n).wait()
        enter(*order[n], first=n == 0)
    loads[2].wait()
    part_load(5).wait()
    pl.semaphore_wait(barrier, 64)

    def iteration(it, carry):
        @pl.when(it > 0)
        def _():
            take_partner(it - 1, 2)

        q, last_rows = qs[o, :, lanes(2)], part_rows(o, 2)
        xq[...] = split(fold(tacc[...] + dot(q, y[last_rows, :], 1, 0)))

        def term(half, pair):
            at = deep(half * 2 + pair)
            v = pacc[:, at] + fold(dot(qs[o, :, lanes(2)], e[last_rows, at], 1, 0) + dot(xq[...], x[:, at], 1, 0))
            return [v[:, 128 * t : 128 * t + 128] for t in range(8)]

        for i in range(2):
            for t, v in enumerate(term(o, pairs[i])):
                pout[it, i, t] = v
            remote(pout.at[it, i], pin.at[it, i], cx_s.at[it], cx_r.at[it, i], partner).start()

        for i in range(2):
            parts = term(c, pairs[i])
            arrived(pin.at[it, i], cx_r.at[it, i])
            for t, v in enumerate(parts):
                pown[it, pairs[i] * 8 + t] = v + pin[it, i, t]
            for dx in pair_offsets[i]:
                to_x = lax.rem(px + dx, 4)
                for dy in far_first:
                    for dz in far_first:
                        if i == 0 or dy or dz or dx is not pair_offsets[1][1]:
                            src = pown.at[it, to_x * 4 + at_y[dy], pl.ds(pl.multiple_of(at_z[dz] * 8, 8), 8), :]
                            slot = slots.at[it, dx * 16 + dy * 4 + dz]
                            to = (at_z[dz] * 2 + c, to_x * 4 + at_y[dy])
                            remote(src, slot, rs_s.at[it], rs_r.at[it], to).start()

        def flip(k, carry):
            for h in range(2):
                et[h, cols(0, k), :] = jnp.transpose(e[half_rows(h), cols(0, k)])
            return carry

        @pl.when(it == 0)
        def _():
            lax.fori_loop(0, 6, flip, 0)

        mine = pl.ds(pl.multiple_of(z * 8, 8), 8)
        slots[it, 0] = pown[it, px * 4 + py, mine, :]
        arrived(slots.at[it, pl.ds(1, 63)], rs_r.at[it])
        pt[it, c, px * 4 + py, mine, :] = jnp.sum(slots[it], axis=0)
        tile = pt.at[it, c, px * 4 + py, mine, :]
        for peer in others:
            remote(tile, tile, ag_s.at[it], ag_r.at[it], chip(*peer)).start()

        def merge(k, carry):
            at = cols(it, k)
            base_o[:, at] = dot(y[...], x[:, at], 1, 0) + e[:, at].astype(F32)
            return carry

        lax.fori_loop(0, 4, merge, 0)

        @pl.when(it == 0)
        def _():
            lax.fori_loop(6, 8, flip, 0)

        arrived(slots.at[it, pl.ds(1, 63)], ag_r.at[it])
        for g in range(2):
            block = pt.at[it, c, pl.ds(8 * g, 8)]
            remote(block, block, fw_s.at[it], fw_r.at[it, g], partner).start()

        def piece(half, g):
            return split(jnp.concatenate([pt[it, half, 8 * g + t] for t in range(8)], axis=1))

        for g in range(2):
            at = deep(2 * c + g)
            p = piece(c, g)
            for h in range(2):
                w = dot(p, et[h, at, :], 1, 0)
                wacc[h] = w if g == 0 else wacc[h] + w
            w = dot(p, x[:, at], 1, 1)
            sacc[...] = w if g == 0 else sacc[...] + w
        for g in range(2):
            arrived(pt.at[it, o, pl.ds(8 * g, 8)], fw_r.at[it, g])
            p = piece(o, g)
            ps[:, g * DEEP : g * DEEP + DEEP] = p
            sacc[...] += dot(p, x[:, deep(2 * o + g)], 1, 1)
        s = split(fold(sacc[...]))

        def finish(h, k):
            at = pl.ds(pl.multiple_of(o * 2048, 2048), 2048)
            w = wacc[h, :, lanes(k)] + dot(ps[...], et[h, at, lanes(k)], 1, 0)
            return fold(w + dot(s, y[part_rows(h, k), :], 1, 1))

        for k in range(3):
            wloc[it, k, :, : PARTS[k][1]] = finish(o, k)
            remote(wloc.at[it, k], wrx.at[it, k], wx_s.at[it], wx_r.at[it, k], partner).start()
        for k in range(3):
            w = finish(c, k)
            arrived(wrx.at[it, k], wx_r.at[it, k])
            wz[it, k, z, :, : PARTS[k][1]] = w + wrx[it, k, :, : PARTS[k][1]]
            mine_z = wz.at[it, k, z]
            for dz in (2, 1, 3):
                remote(mine_z, mine_z, wz_s.at[it], wz_r.at[it, k, dz], chip(0, 0, dz)).start()

        def add_gram(k, total):
            p = split(jnp.concatenate([pt[it, k // 2, (k % 2) * 8 + t] for t in range(8)], axis=1))
            return total + dot(p, p, 1, 1)

        gram = fold(lax.fori_loop(0, 4, add_gram, jnp.zeros((96, 96), F32)))
        gram = gram[:, :32] + (gram[:, 32:64] + gram[:, 64:])
        linv[...] = inverse_factor(gram)

        @pl.when(it == ITERS - 1)
        def _():
            def write_left(k, carry):
                p = jnp.concatenate([pt[it, k // 4, (k % 4) * 4 + t] for t in range(4)], axis=1)
                p = split(-exact(linv[...], p, 1, 0))
                left_o[:, cols(0, k)] = jnp.concatenate([p[:32], p[:32], p[32:64], p[32:64]], axis=0)
                return carry

            lax.fori_loop(0, 8, write_left, 0)

        for k in range(3):
            for dz in (1, 3, 2):
                arrived(wz.at[it, k, at_z[4 - dz]], wz_r.at[it, k, dz])
            total = ((wz[it, k, 0] + wz[it, k, 1]) + wz[it, k, 2]) + wz[it, k, 3]
            wfull[it, c, k] = total
            block = wfull.at[it, c, k]
            remote(block, block, wf_s.at[it], wf_r.at[it, k], partner).start()
            take(it, c, k)

            @pl.when(it < ITERS - 1)
            def _():
                enter(c, k, first=k == 0)
                if k > 0:
                    take_partner(it, k - 1)
                    enter(o, k - 1)

        return carry

    lax.fori_loop(0, ITERS, iteration, 0)
    last = ITERS - 1

    def lay_out(h, k):
        q = qs[h, :64, lanes(k)].astype(F32)
        right_o[part_rows(h, k)] = jnp.transpose(jnp.concatenate([q, q], axis=0)).astype(BF)

    for k in range(3):
        lay_out(c, k)
    for k in range(3):
        take_partner(last, k)
        lay_out(o, k)
    for h in range(2):
        for k in range(3):
            first, width = h * HALF + PARTS[k][0], PARTS[k][1]
            qt_o[:, first : first + width] = exact(0.125 * linv[...], wfull[last, h, k], 1, 0)[:, :width]

    for it in range(ITERS):
        arrived(pout.at[it], cx_s.at[it])
        arrived(slots.at[it, pl.ds(1, 63)], rs_s.at[it])
        arrived(slots.at[it, pl.ds(1, 63)], ag_s.at[it])
        arrived(pt.at[it, c], fw_s.at[it])
        arrived(wrx.at[it], wx_s.at[it])
        arrived(wz.at[it, pl.ds(0, 3), pl.ds(0, 3)], wz_s.at[it])
        arrived(wfull.at[it, c], wf_s.at[it])


def error_kernel(base, left, right, qt, out, q_out, wide, narrow, sem):
    blocks = ((0, 2048, wide), (2048, 1024, narrow.at[0]), (3072, 1024, narrow.at[1]))
    writes = []
    for i, (first, width, stage) in enumerate(blocks):
        at = pl.ds(first, width)
        stage[...] = (base[:, at] + dot(right[...], left[:, at], 1, 0)).astype(BF)
        writes.append(pltpu.make_async_copy(stage, out.at[0, :, at], sem.at[i]))
        writes[i].start()
    q_out[...] = qt[...]
    for write in writes:
        write.wait()


def local(inputs, grad_out, error, q_prev):
    grad_out, q_prev, error = grad_out.T, q_prev.T, jnp.swapaxes(error, 1, 2)
    tokens, dw = inputs.shape
    rank, ff = q_prev.shape
    vmem = pl.BlockSpec(memory_space=pltpu.VMEM)
    anywhere = pl.BlockSpec(memory_space=pl.ANY)
    dma = pltpu.SemaphoreType.DMA
    left, right, qt, base = pl.pallas_call(
        factors_kernel,
        out_shape=(
            pltpu.VMEM((4 * rank, dw), BF),
            pltpu.VMEM((ff, 4 * rank), BF),
            pltpu.VMEM((rank, ff), F32),
            pltpu.VMEM((ff, dw), F32),
        ),
        in_specs=[anywhere] * 4,
        out_specs=(vmem,) * 4,
        scratch_shapes=[
            pltpu.VMEM((tokens, dw), BF),
            pltpu.VMEM((ff, tokens), BF),
            pltpu.VMEM((ff, dw), BF),
            pltpu.VMEM((2, dw, HALF), BF),
            pltpu.VMEM((rank, ff), F32),
            pltpu.VMEM((2, 3 * rank, HALF), BF),
            pltpu.VMEM((3 * rank, 2 * DEEP), BF),
            pltpu.VMEM((3 * rank, tokens), BF),
            pltpu.VMEM((3 * rank, tokens), F32),
            pltpu.VMEM((rank, dw), F32),
            pltpu.VMEM((2, 3 * rank, HALF), F32),
            pltpu.VMEM((3 * rank, tokens), F32),
            pltpu.VMEM((rank, rank), F32),
            pltpu.VMEM((2, 2, 8, rank, 128), F32),
            pltpu.VMEM((2, 2, 8, rank, 128), F32),
            pltpu.VMEM((2, 16, rank, 128), F32),
            pltpu.VMEM((2, 64, 8, 128), F32),
            pltpu.VMEM((2, 2, 16, rank, 128), F32),
            pltpu.VMEM((2, 3, rank, 256), F32),
            pltpu.VMEM((2, 3, rank, 256), F32),
            pltpu.VMEM((2, 3, 4, rank, 256), F32),
            pltpu.VMEM((2, 2, 3, rank, 256), F32),
            dma((3,)), dma((6,)),
            dma((2,)), dma((2, 2)),
            dma((2,)), dma((2,)),
            dma((2,)), dma((2,)),
            dma((2,)), dma((2, 2)),
            dma((2,)), dma((2, 3)),
            dma((2,)), dma((2, 3, 4)),
            dma((2,)), dma((2, 3)),
        ],
        compiler_params=pltpu.CompilerParams(
            collective_id=0, has_side_effects=True, vmem_limit_bytes=36 * 2**20
        ),
        name="power_iterations",
    )(*[pltpu.with_memory_space_constraint(v, pltpu.HBM) for v in (inputs, grad_out, error, q_prev)])
    new_error, q_new = pl.pallas_call(
        error_kernel,
        out_shape=(jax.ShapeDtypeStruct(error.shape, BF), jax.ShapeDtypeStruct((rank, ff), F32)),
        in_specs=[vmem] * 4,
        out_specs=(anywhere, vmem),
        scratch_shapes=[pltpu.VMEM((ff, 2 * DEEP), BF), pltpu.VMEM((2, ff, DEEP), BF), dma((3,))],
        compiler_params=pltpu.CompilerParams(vmem_limit_bytes=24 * 2**20),
        name="new_error",
    )(base, left, right, qt)
    return jnp.swapaxes(new_error, 1, 2), q_new.T


def solution(mesh):
    placed = (P("dp", None), P("dp", "mp"), P("dp", None, "mp"), P("mp", None))
    return jax.shard_map(
        local,
        mesh=mesh,
        in_specs=placed,
        out_specs=(P("dp", None, "mp"), P("mp", None)),
        check_vma=False,
    )
```

```python
import jax
import jax.numpy as jnp
from jax import lax
from jax.experimental import pallas as pl
from jax.experimental.pallas import tpu as pltpu
from jax.sharding import PartitionSpec as P

MESH = pl.DeviceIdType.MESH
BF, F32 = jnp.bfloat16, jnp.float32
ITERS = 2
UNIT = 512
HALF = 688
PARTS = ((0, 256), (256, 256), (512, 176))
DEEP = 1024


def dot(a, b, ca, cb):
    return lax.dot_general(a, b, (((ca,), (cb,)), ((), ())), preferred_element_type=F32)


def exact(a, b, ca, cb):
    return lax.dot_general(
        a, b, (((ca,), (cb,)), ((), ())), precision=lax.Precision.HIGHEST, preferred_element_type=F32
    )


def split(v):
    hi = v.astype(BF)
    rest = v - hi.astype(F32)
    mid = rest.astype(BF)
    low = (rest - mid.astype(F32)).astype(BF)
    return jnp.concatenate([hi, mid, low], axis=0)


def fold(v):
    r = v.shape[0] // 3
    return v[:r] + (v[r : 2 * r] + v[2 * r :])


def inverse_factor(gram):
    r = gram.shape[0]
    row = lax.broadcasted_iota(jnp.int32, (r, 2 * r), 0)
    col = lax.broadcasted_iota(jnp.int32, (r, 2 * r), 1)
    eye = (row == col)[:, :r].astype(F32)
    a = jnp.concatenate([gram, eye], axis=1)
    for j in range(r):
        factor = a[:, j : j + 1] / a[j : j + 1, j : j + 1]
        a = a - jnp.where(row > j, factor, 0.0) * a[j : j + 1, :]
    pivots = jnp.sum(jnp.where(row == col, a, 0.0), axis=1, keepdims=True)
    return a[:, r:] * lax.rsqrt(pivots)


def factors_kernel(
    x_h, y_h, e_h, q0_h, left_o, right_o, qt_o, base_o,
    x, y, e, et, q0, qs, ps, xq, tacc, pacc, wacc, sacc, linv,
    pout, pin, pown, slots, pt, wloc, wrx, wz, wfull,
    in_sem, e_sem, cx_s, cx_r, rs_s, rs_r, ag_s, ag_r, fw_s, fw_r, wx_s, wx_r, wz_s, wz_r, wf_s, wf_r,
):
    dp, mp = lax.axis_index("dp"), lax.axis_index("mp")
    z, c = lax.div(dp, 2), lax.rem(dp, 2)
    px, py = lax.div(mp, 4), lax.rem(mp, 4)
    o = 1 - c
    partner = (z * 2 + o, mp)
    at_x = [lax.rem(px + k, 4) for k in range(4)]
    at_y = [lax.rem(py + k, 4) for k in range(4)]
    at_z = [lax.rem(z + k, 4) for k in range(4)]
    far_first = (2, 1, 3, 0)
    odd = lax.rem(px, 2)
    pairs = (lax.div(at_x[2], 2), 1 - lax.div(at_x[2], 2))
    pair_offsets = ((2, 3 - 2 * odd), (1 + 2 * odd, 0))
    others = [(dx, dy, dz) for dx in far_first for dy in far_first for dz in far_first][:-1]
    others.sort(key=lambda peer: -sum(min(k, 4 - k) for k in peer))

    def chip(dx, dy, dz):
        return (at_z[dz] * 2 + c, at_x[dx] * 4 + at_y[dy])

    def cols(half, u):
        return pl.ds(pl.multiple_of(half * 2048 + u * UNIT, UNIT), UNIT)

    def deep(k):
        return pl.ds(pl.multiple_of(k * DEEP, DEEP), DEEP)

    def half_rows(h):
        return pl.ds(pl.multiple_of(h * HALF, 16), HALF)

    def part_rows(h, k):
        first, width = PARTS[k]
        return pl.ds(pl.multiple_of(h * HALF + first, 16), width)

    def lanes(k):
        return pl.ds(*PARTS[k])

    def remote(src, dst, ss, rs, to):
        return pltpu.make_async_remote_copy(src, dst, ss, rs, device_id=to, device_id_type=MESH)

    def arrived(ref, sem):
        pltpu.make_async_copy(ref, ref, sem).wait()

    barrier = pltpu.get_barrier_semaphore()
    for peer in others:
        pl.semaphore_signal(barrier, inc=1, device_id=chip(*peer), device_id_type=MESH)
    pl.semaphore_signal(barrier, inc=1, device_id=partner, device_id_type=MESH)

    loads = [
        pltpu.make_async_copy(q0_h, q0, in_sem.at[0]),
        pltpu.make_async_copy(y_h, y, in_sem.at[1]),
        pltpu.make_async_copy(x_h, x, in_sem.at[2]),
    ]

    order = ((c, 0), (c, 1), (c, 2), (o, 0), (o, 1), (o, 2))

    def part_load(n):
        at = part_rows(*order[n])
        return pltpu.make_async_copy(e_h.at[0, at, :], e.at[at, :], e_sem.at[n])

    loads[0].start()
    part_load(0).start()
    loads[1].start()
    for n in range(1, 5):
        part_load(n).start()
    loads[2].start()
    part_load(5).start()

    wz[...] = jnp.zeros_like(wz)
    wloc[...] = jnp.zeros_like(wloc)
    loads[0].wait()
    for h in range(2):
        qs[h] = split(q0[:, h * HALF : h * HALF + HALF])

    def enter(h, k, first=False):
        q, at = qs[h, :, lanes(k)], part_rows(h, k)
        t = dot(q, y[at, :], 1, 0)
        tacc[...] = t if first else tacc[...] + t
        for j in range(2):
            to = pl.ds(j * 2048, 2048)
            v = fold(dot(q, e[at, to], 1, 0))
            pacc[:, to] = v if first else pacc[:, to] + v

    def take(it, h, k):
        qs[h, :, lanes(k)] = split(exact(0.125 * linv[...], wfull[it, h, k], 1, 0))[:, : PARTS[k][1]]

    def take_partner(it, k):
        arrived(wfull.at[it, o, k], wf_r.at[it, k])
        take(it, o, k)

    loads[1].wait()
    for n in range(5):
        part_load(n).wait()
        enter(*order[n], first=n == 0)
    loads[2].wait()
    part_load(5).wait()
    pl.semaphore_wait(barrier, 64)

    def iteration(it, carry):
        @pl.when(it > 0)
        def _():
            take_partner(it - 1, 2)

        q, last_rows = qs[o, :, lanes(2)], part_rows(o, 2)
        xq[...] = split(fold(tacc[...] + dot(q, y[last_rows, :], 1, 0)))

        def term(half, pair):
            at = deep(half * 2 + pair)
            v = pacc[:, at] + fold(dot(qs[o, :, lanes(2)], e[last_rows, at], 1, 0) + dot(xq[...], x[:, at], 1, 0))
            return [v[:, 128 * t : 128 * t + 128] for t in range(8)]

        for i in range(2):
            for t, v in enumerate(term(o, pairs[i])):
                pout[it, i, t] = v
            remote(pout.at[it, i], pin.at[it, i], cx_s.at[it], cx_r.at[it, i], partner).start()

        for i in range(2):
            parts = term(c, pairs[i])
            arrived(pin.at[it, i], cx_r.at[it, i])
            for t, v in enumerate(parts):
                pown[it, pairs[i] * 8 + t] = v + pin[it, i, t]
            for dx in pair_offsets[i]:
                to_x = lax.rem(px + dx, 4)
                for dy in far_first:
                    for dz in far_first:
                        if i == 0 or dy or dz or dx is not pair_offsets[1][1]:
                            src = pown.at[it, to_x * 4 + at_y[dy], pl.ds(pl.multiple_of(at_z[dz] * 8, 8), 8), :]
                            slot = slots.at[it, dx * 16 + dy * 4 + dz]
                            to = (at_z[dz] * 2 + c, to_x * 4 + at_y[dy])
                            remote(src, slot, rs_s.at[it], rs_r.at[it], to).start()

        def flip(k, carry):
            for h in range(2):
                et[h, cols(0, k), :] = jnp.transpose(e[half_rows(h), cols(0, k)])
            return carry

        @pl.when(it == 0)
        def _():
            lax.fori_loop(0, 6, flip, 0)

        mine = pl.ds(pl.multiple_of(z * 8, 8), 8)
        slots[it, 0] = pown[it, px * 4 + py, mine, :]
        arrived(slots.at[it, pl.ds(1, 63)], rs_r.at[it])
        pt[it, c, px * 4 + py, mine, :] = jnp.sum(slots[it], axis=0)
        tile = pt.at[it, c, px * 4 + py, mine, :]
        for peer in others:
            remote(tile, tile, ag_s.at[it], ag_r.at[it], chip(*peer)).start()

        def merge(k, carry):
            at = cols(it, k)
            base_o[:, at] = dot(y[...], x[:, at], 1, 0) + e[:, at].astype(F32)
            return carry

        lax.fori_loop(0, 4, merge, 0)

        @pl.when(it == 0)
        def _():
            lax.fori_loop(6, 8, flip, 0)

        arrived(slots.at[it, pl.ds(1, 63)], ag_r.at[it])
        for g in range(2):
            block = pt.at[it, c, pl.ds(8 * g, 8)]
            remote(block, block, fw_s.at[it], fw_r.at[it, g], partner).start()

        def piece(half, g):
            return split(jnp.concatenate([pt[it, half, 8 * g + t] for t in range(8)], axis=1))

        for g in range(2):
            at = deep(2 * c + g)
            p = piece(c, g)
            for h in range(2):
                w = dot(p, et[h, at, :], 1, 0)
                wacc[h] = w if g == 0 else wacc[h] + w
            w = dot(p, x[:, at], 1, 1)
            sacc[...] = w if g == 0 else sacc[...] + w
        for g in range(2):
            arrived(pt.at[it, o, pl.ds(8 * g, 8)], fw_r.at[it, g])
            p = piece(o, g)
            ps[:, g * DEEP : g * DEEP + DEEP] = p
            sacc[...] += dot(p, x[:, deep(2 * o + g)], 1, 1)
        s = split(fold(sacc[...]))

        def finish(h, k):
            at = pl.ds(pl.multiple_of(o * 2048, 2048), 2048)
            w = wacc[h, :, lanes(k)] + dot(ps[...], et[h, at, lanes(k)], 1, 0)
            return fold(w + dot(s, y[part_rows(h, k), :], 1, 1))

        for k in range(3):
            wloc[it, k, :, : PARTS[k][1]] = finish(o, k)
            remote(wloc.at[it, k], wrx.at[it, k], wx_s.at[it], wx_r.at[it, k], partner).start()
        for k in range(3):
            w = finish(c, k)
            arrived(wrx.at[it, k], wx_r.at[it, k])
            wz[it, k, z, :, : PARTS[k][1]] = w + wrx[it, k, :, : PARTS[k][1]]
            mine_z = wz.at[it, k, z]
            for dz in (2, 1, 3):
                remote(mine_z, mine_z, wz_s.at[it], wz_r.at[it, k, dz], chip(0, 0, dz)).start()

        def add_gram(k, total):
            p = split(jnp.concatenate([pt[it, k // 2, (k % 2) * 8 + t] for t in range(8)], axis=1))
            return total + dot(p, p, 1, 1)

        gram = fold(lax.fori_loop(0, 4, add_gram, jnp.zeros((96, 96), F32)))
        gram = gram[:, :32] + (gram[:, 32:64] + gram[:, 64:])
        linv[...] = inverse_factor(gram)

        @pl.when(it == ITERS - 1)
        def _():
            def write_left(k, carry):
                p = jnp.concatenate([pt[it, k // 4, (k % 4) * 4 + t] for t in range(4)], axis=1)
                p = split(-exact(linv[...], p, 1, 0))
                left_o[:, cols(0, k)] = jnp.concatenate([p[:32], p[:32], p[32:64], p[32:64]], axis=0)
                return carry

            lax.fori_loop(0, 8, write_left, 0)

        for k in range(3):
            for dz in (1, 3, 2):
                arrived(wz.at[it, k, at_z[4 - dz]], wz_r.at[it, k, dz])
            total = ((wz[it, k, 0] + wz[it, k, 1]) + wz[it, k, 2]) + wz[it, k, 3]
            wfull[it, c, k] = total
            block = wfull.at[it, c, k]
            remote(block, block, wf_s.at[it], wf_r.at[it, k], partner).start()
            take(it, c, k)

            @pl.when(it < ITERS - 1)
            def _():
                enter(c, k, first=k == 0)
                if k > 0:
                    take_partner(it, k - 1)
                    enter(o, k - 1)

        return carry

    lax.fori_loop(0, ITERS, iteration, 0)
    last = ITERS - 1

    def lay_out(h, k):
        q = qs[h, :64, lanes(k)].astype(F32)
        right_o[part_rows(h, k)] = jnp.transpose(jnp.concatenate([q, q], axis=0)).astype(BF)

    for k in range(3):
        lay_out(c, k)
    for k in range(3):
        take_partner(last, k)
        lay_out(o, k)
    for h in range(2):
        for k in range(3):
            first, width = h * HALF + PARTS[k][0], PARTS[k][1]
            qt_o[:, first : first + width] = exact(0.125 * linv[...], wfull[last, h, k], 1, 0)[:, :width]

    for it in range(ITERS):
        arrived(pout.at[it], cx_s.at[it])
        arrived(slots.at[it, pl.ds(1, 63)], rs_s.at[it])
        arrived(slots.at[it, pl.ds(1, 63)], ag_s.at[it])
        arrived(pt.at[it, c], fw_s.at[it])
        arrived(wrx.at[it], wx_s.at[it])
        arrived(wz.at[it, pl.ds(0, 3), pl.ds(0, 3)], wz_s.at[it])
        arrived(wfull.at[it, c], wf_s.at[it])


def error_kernel(base, left, right, qt, out, q_out, stage, sem):
    writes = []
    for first in range(0, 4096, DEEP):
        at = pl.ds(first, DEEP)
        stage[:, at] = (base[:, at] + dot(right[...], left[:, at], 1, 0)).astype(BF)
        for k in range(4):
            piece = pl.ds(first + k * 256, 256)
            write = pltpu.make_async_copy(stage.at[:, piece], out.at[0, :, piece], sem.at[len(writes)])
            write.start()
            writes.append(write)
    q_out[...] = qt[...]
    for write in writes:
        write.wait()


def local(inputs, grad_out, error, q_prev):
    grad_out, q_prev, error = grad_out.T, q_prev.T, jnp.swapaxes(error, 1, 2)
    tokens, dw = inputs.shape
    rank, ff = q_prev.shape
    vmem = pl.BlockSpec(memory_space=pltpu.VMEM)
    anywhere = pl.BlockSpec(memory_space=pl.ANY)
    dma = pltpu.SemaphoreType.DMA
    left, right, qt, base = pl.pallas_call(
        factors_kernel,
        out_shape=(
            pltpu.VMEM((4 * rank, dw), BF),
            pltpu.VMEM((ff, 4 * rank), BF),
            pltpu.VMEM((rank, ff), F32),
            pltpu.VMEM((ff, dw), F32),
        ),
        in_specs=[anywhere] * 4,
        out_specs=(vmem,) * 4,
        scratch_shapes=[
            pltpu.VMEM((tokens, dw), BF),
            pltpu.VMEM((ff, tokens), BF),
            pltpu.VMEM((ff, dw), BF),
            pltpu.VMEM((2, dw, HALF), BF),
            pltpu.VMEM((rank, ff), F32),
            pltpu.VMEM((2, 3 * rank, HALF), BF),
            pltpu.VMEM((3 * rank, 2 * DEEP), BF),
            pltpu.VMEM((3 * rank, tokens), BF),
            pltpu.VMEM((3 * rank, tokens), F32),
            pltpu.VMEM((rank, dw), F32),
            pltpu.VMEM((2, 3 * rank, HALF), F32),
            pltpu.VMEM((3 * rank, tokens), F32),
            pltpu.VMEM((rank, rank), F32),
            pltpu.VMEM((2, 2, 8, rank, 128), F32),
            pltpu.VMEM((2, 2, 8, rank, 128), F32),
            pltpu.VMEM((2, 16, rank, 128), F32),
            pltpu.VMEM((2, 64, 8, 128), F32),
            pltpu.VMEM((2, 2, 16, rank, 128), F32),
            pltpu.VMEM((2, 3, rank, 256), F32),
            pltpu.VMEM((2, 3, rank, 256), F32),
            pltpu.VMEM((2, 3, 4, rank, 256), F32),
            pltpu.VMEM((2, 2, 3, rank, 256), F32),
            dma((3,)), dma((6,)),
            dma((2,)), dma((2, 2)),
            dma((2,)), dma((2,)),
            dma((2,)), dma((2,)),
            dma((2,)), dma((2, 2)),
            dma((2,)), dma((2, 3)),
            dma((2,)), dma((2, 3, 4)),
            dma((2,)), dma((2, 3)),
        ],
        compiler_params=pltpu.CompilerParams(
            collective_id=0, has_side_effects=True, vmem_limit_bytes=36 * 2**20
        ),
        name="power_iterations",
    )(*[pltpu.with_memory_space_constraint(v, pltpu.HBM) for v in (inputs, grad_out, error, q_prev)])
    new_error, q_new = pl.pallas_call(
        error_kernel,
        out_shape=(jax.ShapeDtypeStruct(error.shape, BF), jax.ShapeDtypeStruct((rank, ff), F32)),
        in_specs=[vmem] * 4,
        out_specs=(anywhere, vmem),
        scratch_shapes=[pltpu.VMEM((ff, dw), BF), dma((16,))],
        compiler_params=pltpu.CompilerParams(vmem_limit_bytes=24 * 2**20),
        name="new_error",
    )(base, left, right, qt)
    return jnp.swapaxes(new_error, 1, 2), q_new.T


def solution(mesh):
    placed = (P("dp", None), P("dp", "mp"), P("dp", None, "mp"), P("mp", None))
    return jax.shard_map(
        local,
        mesh=mesh,
        in_specs=placed,
        out_specs=(P("dp", None, "mp"), P("mp", None)),
        check_vma=False,
    )
```

```python
import jax
import jax.numpy as jnp
from jax import lax
from jax.experimental import pallas as pl
from jax.experimental.pallas import tpu as pltpu
from jax.sharding import PartitionSpec as P

MESH = pl.DeviceIdType.MESH
BF, F32 = jnp.bfloat16, jnp.float32
ITERS = 2
UNIT = 512
HALF = 688
PARTS = ((0, 256), (256, 256), (512, 176))
DEEP = 1024


def dot(a, b, ca, cb):
    return lax.dot_general(a, b, (((ca,), (cb,)), ((), ())), preferred_element_type=F32)


def exact(a, b, ca, cb):
    return lax.dot_general(
        a, b, (((ca,), (cb,)), ((), ())), precision=lax.Precision.HIGHEST, preferred_element_type=F32
    )


def split(v):
    hi = v.astype(BF)
    rest = v - hi.astype(F32)
    mid = rest.astype(BF)
    low = (rest - mid.astype(F32)).astype(BF)
    return jnp.concatenate([hi, mid, low], axis=0)


def fold(v):
    r = v.shape[0] // 3
    return v[:r] + (v[r : 2 * r] + v[2 * r :])


def inverse_factor(gram):
    r = gram.shape[0]
    row = lax.broadcasted_iota(jnp.int32, (r, 2 * r), 0)
    col = lax.broadcasted_iota(jnp.int32, (r, 2 * r), 1)
    eye = (row == col)[:, :r].astype(F32)
    a = jnp.concatenate([gram, eye], axis=1)
    for j in range(r):
        factor = a[:, j : j + 1] / a[j : j + 1, j : j + 1]
        a = a - jnp.where(row > j, factor, 0.0) * a[j : j + 1, :]
    pivots = jnp.sum(jnp.where(row == col, a, 0.0), axis=1, keepdims=True)
    return a[:, r:] * lax.rsqrt(pivots)


def factors_kernel(
    x_h, y_h, e_h, q0_h, left_o, right_o, qt_o, base_o,
    x, y, e, et, q0, qs, ps, xq, tacc, pacc, wacc, sacc, linv,
    pout, pin, pown, slots, pt, wloc, wrx, wz, wfull,
    in_sem, e_sem, cx_s, cx_r, rs_s, rs_r, ag_s, ag_r, fw_s, fw_r, wx_s, wx_r, wz_s, wz_r, wf_s, wf_r,
):
    dp, mp = lax.axis_index("dp"), lax.axis_index("mp")
    z, c = lax.div(dp, 2), lax.rem(dp, 2)
    px, py = lax.div(mp, 4), lax.rem(mp, 4)
    o = 1 - c
    partner = (z * 2 + o, mp)
    at_x = [lax.rem(px + k, 4) for k in range(4)]
    at_y = [lax.rem(py + k, 4) for k in range(4)]
    at_z = [lax.rem(z + k, 4) for k in range(4)]
    far_first = (2, 1, 3, 0)
    odd = lax.rem(px, 2)
    pairs = (lax.div(at_x[2], 2), 1 - lax.div(at_x[2], 2))
    pair_offsets = ((2, 3 - 2 * odd), (1 + 2 * odd, 0))
    others = [(dx, dy, dz) for dx in far_first for dy in far_first for dz in far_first][:-1]
    others.sort(key=lambda peer: -sum(min(k, 4 - k) for k in peer))

    def chip(dx, dy, dz):
        return (at_z[dz] * 2 + c, at_x[dx] * 4 + at_y[dy])

    def cols(half, u):
        return pl.ds(pl.multiple_of(half * 2048 + u * UNIT, UNIT), UNIT)

    def deep(k):
        return pl.ds(pl.multiple_of(k * DEEP, DEEP), DEEP)

    def half_rows(h):
        return pl.ds(pl.multiple_of(h * HALF, 16), HALF)

    def part_rows(h, k):
        first, width = PARTS[k]
        return pl.ds(pl.multiple_of(h * HALF + first, 16), width)

    def lanes(k):
        return pl.ds(*PARTS[k])

    def remote(src, dst, ss, rs, to):
        return pltpu.make_async_remote_copy(src, dst, ss, rs, device_id=to, device_id_type=MESH)

    def arrived(ref, sem):
        pltpu.make_async_copy(ref, ref, sem).wait()

    barrier = pltpu.get_barrier_semaphore()
    for peer in others:
        pl.semaphore_signal(barrier, inc=1, device_id=chip(*peer), device_id_type=MESH)
    pl.semaphore_signal(barrier, inc=1, device_id=partner, device_id_type=MESH)

    loads = [
        pltpu.make_async_copy(q0_h, q0, in_sem.at[0]),
        pltpu.make_async_copy(y_h, y, in_sem.at[1]),
        pltpu.make_async_copy(x_h, x, in_sem.at[2]),
    ]

    order = ((c, 0), (c, 1), (c, 2), (o, 0), (o, 1), (o, 2))

    def part_load(n):
        at = part_rows(*order[n])
        return pltpu.make_async_copy(e_h.at[0, at, :], e.at[at, :], e_sem.at[n])

    loads[0].start()
    part_load(0).start()
    loads[1].start()
    for n in range(1, 5):
        part_load(n).start()
    loads[2].start()
    part_load(5).start()

    wz[...] = jnp.zeros_like(wz)
    wloc[...] = jnp.zeros_like(wloc)
    loads[0].wait()
    for h in range(2):
        qs[h] = split(q0[:, h * HALF : h * HALF + HALF])

    def enter(h, k, first=False):
        q, at = qs[h, :, lanes(k)], part_rows(h, k)
        t = dot(q, y[at, :], 1, 0)
        tacc[...] = t if first else tacc[...] + t
        for j in range(2):
            to = pl.ds(j * 2048, 2048)
            v = fold(dot(q, e[at, to], 1, 0))
            pacc[:, to] = v if first else pacc[:, to] + v

    def take(it, h, k):
        qs[h, :, lanes(k)] = split(exact(0.125 * linv[...], wfull[it, h, k], 1, 0))[:, : PARTS[k][1]]

    def take_partner(it, k):
        arrived(wfull.at[it, o, k], wf_r.at[it, k])
        take(it, o, k)

    loads[1].wait()
    for n in range(5):
        part_load(n).wait()
        enter(*order[n], first=n == 0)
    loads[2].wait()
    part_load(5).wait()
    pl.semaphore_wait(barrier, 64)

    def iteration(it, carry):
        @pl.when(it > 0)
        def _():
            take_partner(it - 1, 2)

        q, last_rows = qs[o, :, lanes(2)], part_rows(o, 2)
        xq[...] = split(fold(tacc[...] + dot(q, y[last_rows, :], 1, 0)))

        def term(half, pair):
            at = deep(half * 2 + pair)
            v = pacc[:, at] + fold(dot(qs[o, :, lanes(2)], e[last_rows, at], 1, 0) + dot(xq[...], x[:, at], 1, 0))
            return [v[:, 128 * t : 128 * t + 128] for t in range(8)]

        for i in range(2):
            for t, v in enumerate(term(o, pairs[i])):
                pout[it, i, t] = v
            remote(pout.at[it, i], pin.at[it, i], cx_s.at[it], cx_r.at[it, i], partner).start()

        for i in range(2):
            parts = term(c, pairs[i])
            arrived(pin.at[it, i], cx_r.at[it, i])
            for t, v in enumerate(parts):
                pown[it, pairs[i] * 8 + t] = v + pin[it, i, t]
            for dx in pair_offsets[i]:
                to_x = lax.rem(px + dx, 4)
                for dy in far_first:
                    for dz in far_first:
                        if i == 0 or dy or dz or dx is not pair_offsets[1][1]:
                            src = pown.at[it, to_x * 4 + at_y[dy], pl.ds(pl.multiple_of(at_z[dz] * 8, 8), 8), :]
                            slot = slots.at[it, dx * 16 + dy * 4 + dz]
                            to = (at_z[dz] * 2 + c, to_x * 4 + at_y[dy])
                            remote(src, slot, rs_s.at[it], rs_r.at[it], to).start()

        def flip(k, carry):
            for h in range(2):
                et[h, cols(0, k), :] = jnp.transpose(e[half_rows(h), cols(0, k)])
            return carry

        @pl.when(it == 0)
        def _():
            lax.fori_loop(0, 6, flip, 0)

        mine = pl.ds(pl.multiple_of(z * 8, 8), 8)
        slots[it, 0] = pown[it, px * 4 + py, mine, :]
        arrived(slots.at[it, pl.ds(1, 63)], rs_r.at[it])
        pt[it, c, px * 4 + py, mine, :] = jnp.sum(slots[it], axis=0)
        tile = pt.at[it, c, px * 4 + py, mine, :]
        for peer in others:
            remote(tile, tile, ag_s.at[it], ag_r.at[it], chip(*peer)).start()

        def merge(k, carry):
            at = cols(it, k)
            base_o[:, at] = dot(y[...], x[:, at], 1, 0) + e[:, at].astype(F32)
            return carry

        lax.fori_loop(0, 4, merge, 0)

        @pl.when(it == 0)
        def _():
            lax.fori_loop(6, 8, flip, 0)

        arrived(slots.at[it, pl.ds(1, 63)], ag_r.at[it])
        for g in range(2):
            block = pt.at[it, c, pl.ds(8 * g, 8)]
            remote(block, block, fw_s.at[it], fw_r.at[it, g], partner).start()

        def piece(half, g):
            return split(jnp.concatenate([pt[it, half, 8 * g + t] for t in range(8)], axis=1))

        for g in range(2):
            at = deep(2 * c + g)
            p = piece(c, g)
            for h in range(2):
                w = dot(p, et[h, at, :], 1, 0)
                wacc[h] = w if g == 0 else wacc[h] + w
            w = dot(p, x[:, at], 1, 1)
            sacc[...] = w if g == 0 else sacc[...] + w
        for g in range(2):
            arrived(pt.at[it, o, pl.ds(8 * g, 8)], fw_r.at[it, g])
            p = piece(o, g)
            ps[:, g * DEEP : g * DEEP + DEEP] = p
            sacc[...] += dot(p, x[:, deep(2 * o + g)], 1, 1)
        s = split(fold(sacc[...]))

        def finish(h, k):
            at = pl.ds(pl.multiple_of(o * 2048, 2048), 2048)
            w = wacc[h, :, lanes(k)] + dot(ps[...], et[h, at, lanes(k)], 1, 0)
            return fold(w + dot(s, y[part_rows(h, k), :], 1, 1))

        for k in range(3):
            wloc[it, k, :, : PARTS[k][1]] = finish(o, k)
            remote(wloc.at[it, k], wrx.at[it, k], wx_s.at[it], wx_r.at[it, k], partner).start()
        for k in range(3):
            w = finish(c, k)
            arrived(wrx.at[it, k], wx_r.at[it, k])
            wz[it, k, z, :, : PARTS[k][1]] = w + wrx[it, k, :, : PARTS[k][1]]
            mine_z = wz.at[it, k, z]
            for dz in (2, 1, 3):
                remote(mine_z, mine_z, wz_s.at[it], wz_r.at[it, k, dz], chip(0, 0, dz)).start()

        def add_gram(k, total):
            p = split(jnp.concatenate([pt[it, k // 2, (k % 2) * 8 + t] for t in range(8)], axis=1))
            return total + dot(p, p, 1, 1)

        gram = fold(lax.fori_loop(0, 4, add_gram, jnp.zeros((96, 96), F32)))
        gram = gram[:, :32] + (gram[:, 32:64] + gram[:, 64:])
        linv[...] = inverse_factor(gram)

        @pl.when(it == ITERS - 1)
        def _():
            def write_left(k, carry):
                p = jnp.concatenate([pt[it, k // 4, (k % 4) * 4 + t] for t in range(4)], axis=1)
                p = split(-exact(linv[...], p, 1, 0))
                left_o[:, cols(0, k)] = jnp.concatenate([p[:32], p[:32], p[32:64], p[32:64]], axis=0)
                return carry

            lax.fori_loop(0, 8, write_left, 0)

        for k in range(3):
            for dz in (1, 3, 2):
                arrived(wz.at[it, k, at_z[4 - dz]], wz_r.at[it, k, dz])
            total = ((wz[it, k, 0] + wz[it, k, 1]) + wz[it, k, 2]) + wz[it, k, 3]
            wfull[it, c, k] = total
            block = wfull.at[it, c, k]
            remote(block, block, wf_s.at[it], wf_r.at[it, k], partner).start()
            take(it, c, k)

            @pl.when(it < ITERS - 1)
            def _():
                enter(c, k, first=k == 0)
                if k > 0:
                    take_partner(it, k - 1)
                    enter(o, k - 1)

        return carry

    lax.fori_loop(0, ITERS, iteration, 0)
    last = ITERS - 1

    def lay_out(h, k):
        q = qs[h, :64, lanes(k)].astype(F32)
        right_o[part_rows(h, k)] = jnp.transpose(jnp.concatenate([q, q], axis=0)).astype(BF)

    for k in range(3):
        lay_out(c, k)
    for k in range(3):
        take_partner(last, k)
        lay_out(o, k)
    for h in range(2):
        for k in range(3):
            first, width = h * HALF + PARTS[k][0], PARTS[k][1]
            qt_o[:, first : first + width] = exact(0.125 * linv[...], wfull[last, h, k], 1, 0)[:, :width]

    for it in range(ITERS):
        arrived(pout.at[it], cx_s.at[it])
        arrived(slots.at[it, pl.ds(1, 63)], rs_s.at[it])
        arrived(slots.at[it, pl.ds(1, 63)], ag_s.at[it])
        arrived(pt.at[it, c], fw_s.at[it])
        arrived(wrx.at[it], wx_s.at[it])
        arrived(wz.at[it, pl.ds(0, 3), pl.ds(0, 3)], wz_s.at[it])
        arrived(wfull.at[it, c], wf_s.at[it])


def error_kernel(base, left, right, qt, out, q_out, stage, sem):
    writes = []
    for first in range(0, 4096, DEEP):
        at = pl.ds(first, DEEP)
        stage[:, at] = (base[:, at] + dot(right[...], left[:, at], 1, 0)).astype(BF)
        for k in range(8):
            piece, rows = pl.ds(first + k // 2 * 256, 256), pl.ds(k % 2 * HALF, HALF)
            write = pltpu.make_async_copy(stage.at[rows, piece], out.at[0, rows, piece], sem.at[len(writes)])
            write.start()
            writes.append(write)
    q_out[...] = qt[...]
    for write in writes:
        write.wait()


def local(inputs, grad_out, error, q_prev):
    grad_out, q_prev, error = grad_out.T, q_prev.T, jnp.swapaxes(error, 1, 2)
    tokens, dw = inputs.shape
    rank, ff = q_prev.shape
    vmem = pl.BlockSpec(memory_space=pltpu.VMEM)
    anywhere = pl.BlockSpec(memory_space=pl.ANY)
    dma = pltpu.SemaphoreType.DMA
    left, right, qt, base = pl.pallas_call(
        factors_kernel,
        out_shape=(
            pltpu.VMEM((4 * rank, dw), BF),
            pltpu.VMEM((ff, 4 * rank), BF),
            pltpu.VMEM((rank, ff), F32),
            pltpu.VMEM((ff, dw), F32),
        ),
        in_specs=[anywhere] * 4,
        out_specs=(vmem,) * 4,
        scratch_shapes=[
            pltpu.VMEM((tokens, dw), BF),
            pltpu.VMEM((ff, tokens), BF),
            pltpu.VMEM((ff, dw), BF),
            pltpu.VMEM((2, dw, HALF), BF),
            pltpu.VMEM((rank, ff), F32),
            pltpu.VMEM((2, 3 * rank, HALF), BF),
            pltpu.VMEM((3 * rank, 2 * DEEP), BF),
            pltpu.VMEM((3 * rank, tokens), BF),
            pltpu.VMEM((3 * rank, tokens), F32),
            pltpu.VMEM((rank, dw), F32),
            pltpu.VMEM((2, 3 * rank, HALF), F32),
            pltpu.VMEM((3 * rank, tokens), F32),
            pltpu.VMEM((rank, rank), F32),
            pltpu.VMEM((2, 2, 8, rank, 128), F32),
            pltpu.VMEM((2, 2, 8, rank, 128), F32),
            pltpu.VMEM((2, 16, rank, 128), F32),
            pltpu.VMEM((2, 64, 8, 128), F32),
            pltpu.VMEM((2, 2, 16, rank, 128), F32),
            pltpu.VMEM((2, 3, rank, 256), F32),
            pltpu.VMEM((2, 3, rank, 256), F32),
            pltpu.VMEM((2, 3, 4, rank, 256), F32),
            pltpu.VMEM((2, 2, 3, rank, 256), F32),
            dma((3,)), dma((6,)),
            dma((2,)), dma((2, 2)),
            dma((2,)), dma((2,)),
            dma((2,)), dma((2,)),
            dma((2,)), dma((2, 2)),
            dma((2,)), dma((2, 3)),
            dma((2,)), dma((2, 3, 4)),
            dma((2,)), dma((2, 3)),
        ],
        compiler_params=pltpu.CompilerParams(
            collective_id=0, has_side_effects=True, vmem_limit_bytes=36 * 2**20
        ),
        name="power_iterations",
    )(*[pltpu.with_memory_space_constraint(v, pltpu.HBM) for v in (inputs, grad_out, error, q_prev)])
    new_error, q_new = pl.pallas_call(
        error_kernel,
        out_shape=(jax.ShapeDtypeStruct(error.shape, BF), jax.ShapeDtypeStruct((rank, ff), F32)),
        in_specs=[vmem] * 4,
        out_specs=(anywhere, vmem),
        scratch_shapes=[pltpu.VMEM((ff, dw), BF), dma((32,))],
        compiler_params=pltpu.CompilerParams(vmem_limit_bytes=24 * 2**20),
        name="new_error",
    )(base, left, right, qt)
    return jnp.swapaxes(new_error, 1, 2), q_new.T


def solution(mesh):
    placed = (P("dp", None), P("dp", "mp"), P("dp", None, "mp"), P("mp", None))
    return jax.shard_map(
        local,
        mesh=mesh,
        in_specs=placed,
        out_specs=(P("dp", None, "mp"), P("mp", None)),
        check_vma=False,
    )
```
